128 devices in a mesh: row: 16 (over z, x_lo, core), col: 8 (over y, x_hi).
Axes of the slice: x: 4 (x_hi: 2, x_lo: 2; x = x_hi * 2 + x_lo), y: 4, z: 4, core: 2. Of those that a mesh axis runs over, the one named last changes fastest.
Arguments:
- voxels: bfloat16 [16, 16, 16384], P('row', 'col'), may hold values from -6 to 6
- norm_gain: float32 [64], replicated, may hold values from 0.25 to 1.75
- in_weight: bfloat16 [64, 256], replicated, may hold values from -0.75 to 0.75
- conv_weight: float32 [6, 4, 128], replicated, may hold values from -3 to 3
- conv_bias: float32 [6, 128], replicated, may hold values from -3 to 3
- x_weight: bfloat16 [6, 128, 36], replicated, may hold values from -0.5 to 0.5
- dt_weight: float32 [6, 4, 128], replicated, may hold values from -3 to 3
- dt_bias: float32 [6, 128], replicated, may hold values from -6 to -1
- a_rate: float32 [6, 128, 16], replicated, may hold values from 0.1 to 4
- skip_gain: float32 [6, 128], replicated, may hold values from 0.5 to 1.5
- out_weight: bfloat16 [128, 64], replicated, may hold values from -0.5 to 0.5
Outputs:
- mixed: bfloat16 [16, 16, 16384], P('row', 'col')
The draws below stay inside these ranges and needn't reach their ends.
All inputs are finite; a program needn't handle non-finite values.
Results may differ from the reference program's by a relative error of at most 0.013.
Values may be sent and summed in bfloat16 or wider, within the bound.
No kernel may reach another device: no remote copies, remote signals or barrier semaphores. Data moves between devices by JAX's collectives and lax.ppermute only.
A program may use at most 64 MiB of HBM per device.

```python
import math
import jax
import jax.numpy as jnp
from jax import lax

C = 64
E = 128
N = 16
R = 4
K = 4
Z = 256
X = 16
Y = 16


def shard_levels(own_key, dims, shards, low, high):
    loudness, own = 1.0, jax.random.fold_in(own_key, 6)
    for axis_at, shards_of in shards:
        steps = jnp.exp(jax.random.uniform(jax.random.fold_in(own, axis_at), (shards_of,), jnp.float32, low / len(shards), high / len(shards)))
        loudness = loudness * jnp.repeat(steps, dims[axis_at] // shards_of).reshape([-1 if axis == axis_at else 1 for axis in range(len(dims))])
    return loudness


def scatter_about(rng, shape, deviation, bound, shards=(), kind=jnp.bfloat16):
    drawn = jax.random.normal(rng, shape, jnp.float32) * deviation
    if len(shards) > 0:
        drawn = shard_levels(rng, shape, shards, -0.22, 0.18) * drawn
    return jnp.clip(drawn, min=-bound, max=bound).astype(kind)


def setup_inputs(seed: int = 0) -> dict:
    key_list = jax.random.split(jax.random.key(seed), 12)
    voxels = scatter_about(key_list[0], (X, Y, Z * C), 1.0, 6.0, ((0, 16), (1, 8)))
    norm_gain = jnp.clip(1.0 + 0.15 * jax.random.normal(key_list[1], (C,), jnp.float32), 0.25, 1.75)
    in_weight = scatter_about(key_list[2], (C, 2 * E), C ** -0.5, 0.75)
    conv_weight = scatter_about(key_list[3], (6, K, E), K ** -0.5, 3.0, (), jnp.float32)
    conv_bias = scatter_about(key_list[4], (6, E), 0.5, 3.0, (), jnp.float32)
    x_weight = scatter_about(key_list[5], (6, E, R + 2 * N), E ** -0.5, 0.5)
    dt_weight = scatter_about(key_list[6], (6, R, E), R ** -0.5, 3.0, (), jnp.float32)
    dt_bias = jnp.clip(jax.random.uniform(key_list[7], (6, E), jnp.float32, -6.0, -1.0), -6.0, -1.0)
    a_rate = jnp.clip(jnp.exp(jax.random.uniform(key_list[8], (6, E, N), jnp.float32, math.log(0.1), math.log(4.0))), 0.1, 4.0)
    skip_gain = jnp.clip(jax.random.uniform(key_list[9], (6, E), jnp.float32, 0.5, 1.5), 0.5, 1.5)
    out_weight = scatter_about(key_list[10], (E, C), E ** -0.5, 0.5)
    return {"voxels": voxels, "norm_gain": norm_gain, "in_weight": in_weight, "conv_weight": conv_weight, "conv_bias": conv_bias, "x_weight": x_weight, "dt_weight": dt_weight, "dt_bias": dt_bias, "a_rate": a_rate, "skip_gain": skip_gain, "out_weight": out_weight}


def activation(line_rows, index, conv_weight, conv_bias):
    kernel = conv_weight.shape[1]
    length = line_rows.shape[1]
    values = line_rows.astype(jnp.float32)
    padded = jnp.pad(values, ((0, 0), (kernel - 1, 0), (0, 0)))
    preact = conv_bias[index].astype(jnp.float32)
    for offset in range(kernel):
        preact = preact + conv_weight[index, offset] * padded[:, offset:offset + length]
    return jax.nn.silu(preact).astype(jnp.bfloat16)

def run_direction(line_rows, index, reverse, conv_weight, conv_bias, x_weight, dt_weight, dt_bias, a_rate, skip_gain):
    ordered = line_rows[:, ::-1] if reverse else line_rows
    activated = activation(ordered, index, conv_weight, conv_bias)
    state_n = a_rate.shape[2]
    rank = dt_weight.shape[1]
    projected = jnp.einsum('mle,ef->mlf', activated.astype(jnp.float32), x_weight[index].astype(jnp.float32))
    low_rank = projected[..., :rank]
    b_select = projected[..., rank:rank + state_n]
    c_select = projected[..., rank + state_n:]
    step_size = jax.nn.softplus(jnp.einsum('mlr,re->mle', low_rank, dt_weight[index], precision=lax.Precision.HIGHEST) + dt_bias[index])
    decay_rate = a_rate[index]
    act_float = activated.astype(jnp.float32)

    def advance(carried, inputs):
        step_now, act_now, b_now, c_now = inputs
        decays = jnp.exp(-step_now[:, :, None] * decay_rate)
        carried = decays * carried + (step_now * act_now)[:, :, None] * b_now[:, None, :]
        return (carried, lax.optimization_barrier(jnp.sum(carried * c_now[:, None, :], axis=2)))
    inputs = (jnp.swapaxes(step_size, 0, 1), jnp.swapaxes(act_float, 0, 1), jnp.swapaxes(b_select, 0, 1), jnp.swapaxes(c_select, 0, 1))
    start = jnp.zeros((line_rows.shape[0], line_rows.shape[2], state_n), jnp.float32)
    _, results = lax.scan(advance, start, inputs)
    results = jnp.swapaxes(results, 0, 1) + skip_gain[index] * act_float
    return results[:, ::-1] if reverse else results

def both_ways(line_rows, index, *params):
    return run_direction(line_rows, index, False, *params) + run_direction(line_rows, index + 1, True, *params)

def reference(voxels, norm_gain, in_weight, conv_weight, conv_bias, x_weight, dt_weight, dt_bias, a_rate, skip_gain, out_weight):
    params = (conv_weight, conv_bias, x_weight, dt_weight, dt_bias, a_rate, skip_gain)
    values = voxels.reshape(X, Y, Z, C).astype(jnp.float32)
    normed = (values * lax.rsqrt(lax.optimization_barrier(jnp.mean(values * values, axis=-1, keepdims=True)) + 1e-05) * norm_gain).astype(jnp.bfloat16)
    flat_rows = normed.reshape(-1, C)
    inner = jnp.dot(flat_rows, in_weight[:, :E], preferred_element_type=jnp.float32).astype(jnp.bfloat16).reshape(X, Y, Z, E)
    gate = jnp.dot(flat_rows, in_weight[:, E:], preferred_element_type=jnp.float32)
    silu_gate = jax.nn.silu(gate)
    along_z = both_ways(inner.reshape(X * Y, Z, E), 0, *params).reshape(X, Y, Z, E)
    along_y = both_ways(inner.transpose(0, 2, 1, 3).reshape(X * Z, Y, E), 2, *params)
    sum_y = along_y.reshape(X, Z, Y, E).transpose(0, 2, 1, 3).astype(jnp.bfloat16)
    along_x = both_ways(inner.transpose(1, 2, 0, 3).reshape(Y * Z, X, E), 4, *params)
    along_x = along_x.reshape(Y, Z, X, E).transpose(2, 0, 1, 3)
    sum_xy = (sum_y.astype(jnp.float32) + along_x).astype(jnp.bfloat16)
    far_hidden = (sum_xy.reshape(-1, E).astype(jnp.float32) * silu_gate).astype(jnp.bfloat16)
    far_part = jnp.dot(far_hidden, out_weight, preferred_element_type=jnp.float32).astype(jnp.bfloat16)
    near_hidden = (along_z.reshape(-1, E) * silu_gate).astype(jnp.bfloat16)
    mixed = (jnp.dot(near_hidden, out_weight, preferred_element_type=jnp.float32) + far_part.astype(jnp.float32)).astype(jnp.bfloat16)
    return mixed.reshape(X, Y, Z * C)
```

```python
import functools
import math

import jax
import jax.numpy as jnp
from jax import lax
from jax.experimental import pallas as pl
from jax.experimental.pallas import tpu as pltpu
from jax.sharding import PartitionSpec as P

C = 64
E = 128
N = 16
R = 4
K = 4
Q = 4
EQ = E // Q
STEPS = 16
LINES = 32
A0, CW0, CB0, DW0, DB0, SK0, ROWS = 0, 16, 20, 21, 25, 26, 27
LOG2E = math.log2(math.e)
F32 = jnp.float32
BF16 = jnp.bfloat16
HIGHEST = lax.Precision.HIGHEST
NT = (((1,), (1,)), ((), ()))
VMEM_LIMIT = 48 * 1024 * 1024


def iota(shape, axis):
    return lax.broadcasted_iota(jnp.int32, shape, axis)


def silu(x):
    half = 0.5 * x
    return half * (1.0 + jnp.tanh(half))


def softplus(x):
    tail = jnp.exp2(jnp.abs(x) * (-LOG2E))
    return jnp.maximum(x, 0.0) + jnp.where(tail < 1e-4, tail, jnp.log(1.0 + tail))


def prepare_kernel(in_w, conv_w, conv_b, x_w, dt_w, dt_b, a_rate, skip, out_w, gain, table, lhsq, xp, wo, gain2):
    mask = ((iota((EQ, E), 1) % EQ) == iota((EQ, E), 0)).astype(F32)
    same = (iota((E, E), 0) // EQ == iota((E, E), 1) // EQ).astype(F32)
    eye = (iota((N, N), 0) == iota((N, N), 1)).astype(F32)
    row, column = iota((40, 36), 0), iota((40, 36), 1)
    pick = (column == jnp.where(row < 2 * N, row + R, row - 2 * N)) & (row < 2 * N + R)
    pick = pick.astype(BF16)
    for d in range(6):
        rates = lax.dot_general(eye, a_rate[d], NT, precision=HIGHEST, preferred_element_type=F32)
        rows = jnp.concatenate(
            [
                rates * (-LOG2E),
                conv_w[d],
                conv_b[d : d + 1, :],
                dt_w[d],
                dt_b[d : d + 1, :],
                skip[d : d + 1, :],
            ],
            axis=0,
        )
        spread = (rows[:, None, :] * mask[None]).reshape(ROWS * EQ, E)
        table[d] = jnp.dot(spread, same, precision=HIGHEST, preferred_element_type=F32).reshape(ROWS, EQ, E)
        xp[d] = lax.dot_general(pick, x_w[d], NT, preferred_element_type=F32).astype(BF16)
    turned = in_w[...].astype(F32).T
    for part in range(2):
        blocks = [turned[part * E + q * EQ : part * E + (q + 1) * EQ] for q in range(Q)]
        lhsq[part * EQ : (part + 1) * EQ, :] = jnp.concatenate(blocks, axis=1).astype(BF16)
    wide = jnp.concatenate([out_w[...], out_w[...]], axis=1)
    low = iota((EQ, 2 * C), 1) < C
    zero = jnp.zeros((EQ, 2 * C), BF16)
    for q in range(Q):
        block = wide[q * EQ : (q + 1) * EQ]
        wo[q, 0] = jnp.where(low, block, zero)
        wo[q, 1] = jnp.where(low, zero, block)
    gain2[...] = jnp.concatenate([gain[...], gain[...]], axis=1)


def normalise(values, gain2, plain, rolled):
    low = iota(values.shape, 1) < C
    squares = values * values
    first = jnp.sum(jnp.where(low, squares, 0.0), axis=1, keepdims=True) * (1.0 / C)
    second = jnp.sum(jnp.where(low, 0.0, squares), axis=1, keepdims=True) * (1.0 / C)
    scale = jnp.where(low, lax.rsqrt(first + 1e-05), lax.rsqrt(second + 1e-05))
    normed = (values * scale * gain2).astype(BF16).astype(F32)
    plain[...] = normed
    rolled[...] = pltpu.roll(normed, C, 1)


def project(blocks, lhsq):
    half = jnp.concatenate(blocks, axis=0)
    zero = jnp.zeros_like(half)
    rows = jnp.concatenate(
        [jnp.concatenate([half, zero], axis=1), jnp.concatenate([zero, half], axis=1)], axis=0
    ).astype(BF16)
    both = lax.dot_general(lhsq, rows, NT, preferred_element_type=F32)
    return both[:EQ].astype(BF16).astype(F32), both[EQ:]


def step_inputs(d, index, neighbours, table, xp, quarter, act_s, sel_s, step_s, fresh_s):
    pre = table[index, CB0]
    for k in range(K):
        if neighbours[k] is not None:
            pre = pre + table[index, CW0 + k] * neighbours[k]
    act = silu(pre).astype(BF16).astype(F32)
    spread = jnp.concatenate([jnp.where(quarter == q, act, 0.0) for q in range(Q)], axis=0).astype(BF16)
    sel = jnp.dot(xp[index], spread, preferred_element_type=F32)
    sel = sel + pltpu.roll(sel, 64, 1)
    sel = sel + pltpu.roll(sel, 32, 1)
    raw = table[index, DB0]
    for r in range(R):
        raw = raw + table[index, DW0 + r] * sel[2 * N + r : 2 * N + r + 1, :]
    step = softplus(raw)
    return act, sel, step


def scan_group(index, d, rows, start, table, sel_s, step_s, fresh_s, y_s):
    rates = [table[index, A0 + n, rows, :] for n in range(N)]
    state = start
    for s in range(STEPS):
        t = s if d == 0 else STEPS - 1 - s
        step = step_s[d, t, rows, :]
        fresh = fresh_s[d, t, rows, :]
        total = [None, None]
        following = []
        for n in range(N):
            new = fresh * sel_s[d, t, n : n + 1, :]
            if state is not None:
                new = new + jnp.exp2(step * rates[n]) * state[n]
            following.append(new)
            term = new * sel_s[d, t, N + n : N + n + 1, :]
            total[n % 2] = term if total[n % 2] is None else total[n % 2] + term
        state = following
        y_s[t, rows, :] = y_s[t, rows, :] + (total[0] + total[1])
    return state


def gated_rows(y_s, gate_s, turned_s):
    for t in range(STEPS):
        turned_s[t] = (y_s[t] * gate_s[t]).T


def plane_kernel(values, table, lhsq_ref, xp, wo, gain2, out, plain, rolled, inner_s, gate_s, act_s, sel_s, step_s, fresh_s, y_s, turned_s, far_s):
    normalise(values[...].astype(F32), gain2[...], plain, rolled)
    quarter = iota((EQ, E), 1) // LINES
    low = iota((STEPS, 2 * C), 1) < C
    lhsq = lhsq_ref[...]
    for axis in range(2):
        for t in range(STEPS):
            where = pl.ds(t, STEPS, stride=STEPS) if axis == 0 else pl.ds(t * STEPS, STEPS)
            own, swapped = plain[where, :], rolled[where, :]
            blocks = [
                jnp.where(low, own, 0.0),
                jnp.where(low, swapped, 0.0),
                jnp.where(low, 0.0, swapped),
                jnp.where(low, 0.0, own),
            ]
            inner, gate = project(blocks, lhsq)
            inner_s[t] = inner
            gate_s[t] = silu(gate)
        for d in range(2):
            index = 2 + 2 * axis + d
            for t in range(STEPS):
                near = [t - 3 + k if d == 0 else t + 3 - k for k in range(K)]
                near = [inner_s[p] if 0 <= p < STEPS else None for p in near]
                act, sel, step = step_inputs(d, index, near, table, xp, quarter, act_s, sel_s, step_s, fresh_s)
                sel_s[d, t] = sel
                step_s[d, t] = step
                fresh_s[d, t] = step * act
                direct = table[index, SK0] * act
                y_s[t] = direct if d == 0 else y_s[t] + direct

        def group(g, carry):
            rows = pl.ds(pl.multiple_of(g * 8, 8), 8)
            for d in range(2):
                scan_group(2 + 2 * axis + d, d, rows, None, table, sel_s, step_s, fresh_s, y_s)
            return carry

        lax.fori_loop(0, EQ // 8, group, 0)
        gated_rows(y_s, gate_s, turned_s)
        far = None
        for q in range(Q):
            for half in range(2):
                first = (2 * q + half) * STEPS
                lhs = turned_s[:, first : first + STEPS, :].reshape(STEPS * STEPS, EQ).astype(BF16)
                part = jnp.dot(lhs, wo[q, half], preferred_element_type=F32)
                far = part if far is None else far + part
        if axis == 0:
            for t in range(STEPS):
                far_s[pl.ds(t, STEPS, stride=STEPS), :] = far[t * STEPS : (t + 1) * STEPS]
        else:
            out[...] = (far + far_s[...]).astype(BF16)


def line_kernel(values, table, lhsq_ref, xp, wo, gain2, out, plain, rolled, inner_s, gate_s, act_s, sel_s, step_s, fresh_s, y_s, turned_s, end_s):
    normalise(values[...].astype(F32), gain2[...], plain, rolled)
    lane = iota((EQ, E), 1)
    quarter = lane // LINES
    chunk = lane % STEPS
    low = iota((STEPS, 2 * C), 1) < C
    lhsq = lhsq_ref[...]
    for t in range(STEPS):
        blocks = []
        for half in range(2):
            for y in range(2):
                where = pl.ds(y * 128 + t // 2, STEPS, stride=8)
                rows = plain[where, :] if t % 2 == half else rolled[where, :]
                blocks.append(jnp.where(low, rows, 0.0) if half == 0 else jnp.where(low, 0.0, rows))
        inner, gate = project(blocks, lhsq)
        inner_s[t] = inner
        gate_s[t] = silu(gate)
    for d in range(2):
        edge = (chunk >= 1) if d == 0 else (chunk < STEPS - 1)
        for t in range(STEPS):
            near = []
            for k in range(K):
                p = t - 3 + k if d == 0 else t + 3 - k
                if 0 <= p < STEPS:
                    near.append(inner_s[p])
                else:
                    moved = pltpu.roll(inner_s[p % STEPS], 1 if d == 0 else E - 1, 1)
                    near.append(jnp.where(edge, moved, 0.0))
            act, sel, step = step_inputs(d, d, near, table, xp, quarter, act_s, sel_s, step_s, fresh_s)
            sel_s[d, t] = sel
            step_s[d, t] = step
            fresh_s[d, t] = step * act
            direct = table[d, SK0] * act
            y_s[t] = direct if d == 0 else y_s[t] + direct

    far_off = 1e4

    def group(g, carry):
        rows = pl.ds(pl.multiple_of(g * 8, 8), 8)
        place = iota((8, E), 1) % STEPS
        for d in range(2):
            rates = [table[d, A0 + n, rows, :] for n in range(N)]
            ends = None
            whole = None
            for s in range(STEPS):
                t = s if d == 0 else STEPS - 1 - s
                step = step_s[d, t, rows, :]
                fresh = fresh_s[d, t, rows, :]
                whole = step if whole is None else whole + step
                following = []
                for n in range(N):
                    new = fresh * sel_s[d, t, n : n + 1, :]
                    if ends is not None:
                        new = new + jnp.exp2(step * rates[n]) * ends[n]
                    following.append(new)
                ends = following
            for k in (1, 2, 4, 8):
                by = k if d == 0 else E - k
                inside = (place >= k) if d == 0 else (place < STEPS - k)
                span = jnp.where(inside, whole, far_off)
                ends = [e + jnp.exp2(span * a) * pltpu.roll(e, by, 1) for e, a in zip(ends, rates)]
                whole = whole + jnp.where(inside, pltpu.roll(whole, by, 1), 0.0)
            by = 1 if d == 0 else E - 1
            inside = (place >= 1) if d == 0 else (place < STEPS - 1)
            start = [jnp.where(inside, pltpu.roll(e, by, 1), 0.0) for e in ends]
            scan_group(d, d, rows, start, table, sel_s, step_s, fresh_s, y_s)
        return carry

    lax.fori_loop(0, EQ // 8, group, 0)
    gated_rows(y_s, gate_s, turned_s)
    near = None
    for q in range(Q):
        for half in range(2):
            steps = [turned_s[2 * p + half, q * LINES : (q + 1) * LINES, :] for p in range(8)]
            lhs = jnp.concatenate(steps, axis=0).astype(BF16)
            part = jnp.dot(lhs, wo[q, half], preferred_element_type=F32)
            near = part if near is None else near + part
    for p in range(8):
        for y in range(2):
            first = p * LINES + y * STEPS
            out[pl.ds(2 * p + y, STEPS, stride=16), :] = near[first : first + STEPS]


def vmem(count):
    return [pl.BlockSpec(memory_space=pltpu.VMEM)] * count


def scan_scratch():
    return [
        pltpu.VMEM((256, E), F32),
        pltpu.VMEM((256, E), F32),
        pltpu.VMEM((STEPS, EQ, E), F32),
        pltpu.VMEM((STEPS, EQ, E), F32),
        pltpu.VMEM((2, STEPS, EQ, E), F32),
        pltpu.VMEM((2, STEPS, 40, E), F32),
        pltpu.VMEM((2, STEPS, EQ, E), F32),
        pltpu.VMEM((2, STEPS, EQ, E), F32),
        pltpu.VMEM((STEPS, EQ, E), F32),
        pltpu.VMEM((STEPS, E, EQ), F32),
    ]


PARAMS = pltpu.CompilerParams(vmem_limit_bytes=VMEM_LIMIT)


def prepare(*weights):
    shapes = [
        jax.ShapeDtypeStruct((6, ROWS, EQ, E), F32),
        jax.ShapeDtypeStruct((2 * EQ, Q * C), BF16),
        jax.ShapeDtypeStruct((6, 40, E), BF16),
        jax.ShapeDtypeStruct((Q, 2, EQ, 2 * C), BF16),
        jax.ShapeDtypeStruct((1, 2 * C), F32),
    ]
    return pl.pallas_call(
        prepare_kernel, out_shape=shapes, in_specs=vmem(10), out_specs=vmem(5), compiler_params=PARAMS, name="prepare"
    )(*weights)


def planes(values, ready):
    return pl.pallas_call(
        plane_kernel,
        out_shape=jax.ShapeDtypeStruct((256, 2 * C), BF16),
        in_specs=vmem(6),
        out_specs=vmem(1)[0],
        scratch_shapes=scan_scratch() + [pltpu.VMEM((256, 2 * C), F32)],
        compiler_params=PARAMS,
        name="planes",
    )(values, *ready)


def z_lines(values, ready):
    return pl.pallas_call(
        line_kernel,
        out_shape=jax.ShapeDtypeStruct((256, 2 * C), F32),
        in_specs=vmem(6),
        out_specs=vmem(1)[0],
        scratch_shapes=scan_scratch() + [pltpu.VMEM((8, E), F32)],
        compiler_params=PARAMS,
        name="z_lines",
    )(values, *ready)


def local(voxels, norm_gain, in_weight, conv_weight, conv_bias, x_weight, dt_weight, dt_bias, a_rate, skip_gain, out_weight):
    pairs = voxels.reshape(2, 128, 2 * C)
    sent = pairs.transpose(1, 0, 2)
    arrived = lax.all_to_all(sent, ("row", "col"), split_axis=0, concat_axis=0, tiled=True)
    ready = prepare(
        in_weight, conv_weight, conv_bias, x_weight, dt_weight, dt_bias, a_rate, skip_gain, out_weight, norm_gain.reshape(1, C)
    )
    far = planes(arrived.reshape(256, 2 * C), ready)
    returned = lax.all_to_all(far.reshape(128, 2, 2 * C), ("row", "col"), split_axis=0, concat_axis=0, tiled=True)
    near = z_lines(pairs.reshape(256, 2 * C), ready)
    mixed = (near.reshape(128, 2, 2 * C) + returned.astype(F32)).astype(BF16)
    return mixed.transpose(1, 0, 2).reshape(1, 2, 128 * 2 * C)


def solution(mesh):
    in_specs = (P("row", "col", None),) + (P(),) * 10
    return jax.shard_map(local, mesh=mesh, in_specs=in_specs, out_specs=P("row", "col", None), check_vma=False)
```

```python
import math

import jax
import jax.numpy as jnp
from jax import lax
from jax.experimental import pallas as pl
from jax.experimental.pallas import tpu as pltpu
from jax.sharding import PartitionSpec as P

C = 64
E = 128
N = 16
R = 4
K = 4
PAD = 8
CW, CB, DB, SK, VEC = 0, 4, 5, 6, 8
Q = 4
EQ = E // Q
STEPS = 16
LINES = 32
A0, CW0, DW0, CB0, DB0, SK0, ROWS = 0, 16, 20, 24, 25, 26, 32
LN2 = math.log(2.0)
LOG2E = 1.0 / LN2
F32 = jnp.float32
BF16 = jnp.bfloat16
HIGHEST = lax.Precision.HIGHEST
NT = (((1,), (1,)), ((), ()))
TN = (((0,), (0,)), ((), ()))
PARAMS = pltpu.CompilerParams(vmem_limit_bytes=48 * 1024 * 1024)


def iota(shape, axis):
    return lax.broadcasted_iota(jnp.int32, shape, axis)


def silu(x):
    half = 0.5 * x
    return half * (1.0 + jnp.tanh(half))


def softplus2(x):
    tail = jnp.exp2(-jnp.abs(x))
    return jnp.maximum(x, 0.0) + jnp.where(tail < 1e-4, tail * LOG2E, jnp.log2(1.0 + tail))


def prepare_kernel(*refs):
    given, (vec, rate_far, w_step, w_in, w_out, gain2, swap), (table, lhsq, xp, wo) = refs[:10], refs[10:17], refs[17:21]
    here, sem = refs[21:31], refs[31]
    copies = [pltpu.make_async_copy(a, b, sem.at[i]) for i, (a, b) in enumerate(zip(given, here))]
    for copy in copies:
        copy.start()
    for copy in copies:
        copy.wait()
    in_w, conv_w, conv_b, x_w, dt_w, dt_b, rate, skip, out_w, gain = here
    row, column = iota((R + 2 * N, E), 0), iota((R + 2 * N, E), 1)
    pick = (row == column % (2 * N) + R).astype(F32)
    for d in range(2, 6):
        vec[d, CW : CW + K] = conv_w[d]
        vec[d, CB : CB + 1] = conv_b[d : d + 1, :]
        vec[d, DB : DB + 1] = dt_b[d : d + 1, :] * LOG2E
        vec[d, SK : SK + 1] = skip[d : d + 1, :]
        vec[d, SK + 1 :] = jnp.zeros((1, E), F32)
        given_w = x_w[d].astype(F32)
        both = lax.dot_general(given_w[:R], dt_w[d] * LOG2E, TN, precision=HIGHEST, preferred_element_type=F32)
        high = both.astype(BF16)
        w_step[d, 0:E, 0:E] = high
        w_step[d, E:, 0:E] = (both - high.astype(F32)).astype(BF16)
        w_step[d, 0:E, E:] = lax.dot_general(given_w, pick, TN, preferred_element_type=F32).astype(BF16)
        w_step[d, E:, E:] = jnp.zeros((E, E), BF16)
    row, column = iota((256, 256), 0), iota((256, 256), 1)
    swap[...] = (column == row % 16 * 16 + row // 16).astype(BF16)
    turned = jnp.concatenate([-rate[2 + i] for i in range(4)], axis=0).T
    high = turned.astype(BF16)
    both = jnp.concatenate([high, (turned - high.astype(F32)).astype(BF16)], axis=1)
    row, column = iota((8 * N, E), 0), iota((8 * N, E), 1)
    for n in range(N):
        chosen = ((row % N == n) & (row // N % 4 == column // 32)).astype(BF16)
        rate_far[n] = jnp.dot(both, chosen, preferred_element_type=F32)
    weight = in_w[...]
    zero = jnp.zeros((C, E), BF16)
    inner, gate = weight[:, :E], weight[:, E:]
    w_in[0:C] = jnp.concatenate([inner, zero, gate, zero], axis=1)
    w_in[C:] = jnp.concatenate([zero, inner, zero, gate], axis=1)
    turned = out_w[...].astype(F32)
    wide = jnp.concatenate([turned, turned], axis=0).T
    low_half = iota((E, 2 * C), 1) < C
    w_out[0:E] = jnp.where(low_half, wide, 0.0).astype(BF16)
    w_out[E:] = jnp.where(low_half, 0.0, wide).astype(BF16)
    gain2[...] = jnp.concatenate([gain[...], gain[...]], axis=1)
    mask = ((iota((EQ, E), 1) % EQ) == iota((EQ, E), 0)).astype(BF16)
    same = (iota((2 * E, E), 0) % E // EQ == iota((2 * E, E), 1) // EQ).astype(BF16)
    row, column = iota((40, 36), 0), iota((40, 36), 1)
    pick = (column == jnp.where(row < 2 * N, row + R, row - 2 * N)) & (row < 2 * N + R)
    pick = pick.astype(BF16)
    for d in range(2):
        rows = jnp.concatenate(
            [
                rate[d] * (-LOG2E),
                conv_w[d],
                dt_w[d],
                conv_b[d : d + 1, :],
                dt_b[d : d + 1, :],
                skip[d : d + 1, :],
                jnp.zeros((5, E), F32),
            ],
            axis=0,
        )
        high = rows.astype(BF16)
        rest = (rows - high.astype(F32)).astype(BF16)
        spread = jnp.concatenate(
            [(part[:, None, :] * mask[None]).reshape(ROWS * EQ, E) for part in (high, rest)], axis=1
        )
        table[d] = jnp.dot(spread, same, preferred_element_type=F32).reshape(ROWS, EQ, E)
        xp[d] = jnp.dot(pick, x_w[d], preferred_element_type=F32).astype(BF16)
    turned = in_w[...].astype(F32).T
    for part in range(2):
        blocks = [turned[part * E + q * EQ : part * E + (q + 1) * EQ] for q in range(Q)]
        lhsq[part * EQ : (part + 1) * EQ, :] = jnp.concatenate(blocks, axis=1).astype(BF16)
    for q in range(Q):
        for half in range(2):
            wo[q, half] = w_out[half * E + q * EQ : half * E + (q + 1) * EQ, :]


def enter(values, gain2, w_in):
    low = iota(values.shape, 1) < C
    squares = values * values
    first = jnp.sum(jnp.where(low, squares, 0.0), axis=1, keepdims=True) * (1.0 / C)
    second = jnp.sum(jnp.where(low, 0.0, squares), axis=1, keepdims=True) * (1.0 / C)
    scale = jnp.where(low, lax.rsqrt(first + 1e-05), lax.rsqrt(second + 1e-05))
    normed = (values * scale * gain2).astype(BF16)
    both = jnp.dot(normed, w_in, preferred_element_type=F32)
    inner = [both[:, h * E : (h + 1) * E].astype(BF16).astype(F32) for h in range(2)]
    gates = [silu(both[:, (2 + h) * E : (3 + h) * E]) for h in range(2)]
    return inner, gates


def leave(first, second, w_out):
    hidden = jnp.concatenate([first.astype(BF16), second.astype(BF16)], axis=1)
    return jnp.dot(hidden, w_out, preferred_element_type=F32)


def step_inputs(taps, vec, w_step):
    pre = vec[CB : CB + 1, :]
    for k in range(K):
        pre = pre + vec[CW + k : CW + k + 1, :] * taps[k]
    act = silu(pre).astype(BF16)
    both = jnp.dot(jnp.concatenate([act, act], axis=1), w_step, preferred_element_type=F32)
    return act.astype(F32), softplus2(both[:, :E] + vec[DB : DB + 1, :]), both[:, E:]


def tree_sum(terms):
    while len(terms) > 1:
        terms = [terms[i] + terms[i + 1] for i in range(0, len(terms), 2)]
    return terms[0]


def plane_kernel(values, vec, rate_far, w_step, w_in, w_out, gain2, swap, out, lines_s, gate_s, step_s, fresh_s, sel_s, step_t, fresh_t, sel_t, y_s, sum_s):
    inner, gates = enter(values[...].astype(F32), gain2[...], w_in[...])
    swapped = jnp.dot(swap[...], jnp.concatenate(inner, axis=1).astype(BF16), preferred_element_type=F32)
    zero = jnp.zeros((96, E), F32)
    for axis in range(2):
        lines_s[axis, 0:96, :] = zero
        lines_s[axis, 608:704, :] = zero
    for h in range(2):
        gate_s[h] = gates[h]
        for i in range(16):
            first = 96 + i * 32 + h * 16
            lines_s[1, first : first + 16, :] = inner[h][i * 16 : (i + 1) * 16]
            lines_s[0, first : first + 16, :] = swapped[i * 16 : (i + 1) * 16, h * E : (h + 1) * E]

    for axis in range(2):
        total = None
        for d in range(2):
            index = 2 + 2 * axis + d
            firsts = [32 * (k if d == 0 else 6 - k) for k in range(K)]
            taps = [lines_s[axis, first : first + 512, :] for first in firsts]
            act, step, sel = step_inputs(taps, vec[index], w_step[index])
            direct = vec[index, SK : SK + 1, :] * act
            total = direct if total is None else total + direct
            fresh = step * act
            rows = slice(axis * 64 + d * 32, axis * 64 + d * 32 + 32)
            for s in range(16):
                t = s if d == 0 else 15 - s
                lanes = slice(s % 4 * 32, s % 4 * 32 + 32)
                step_s[s, rows, :] = step[t * 32 : (t + 1) * 32]
                fresh_s[s, rows, :] = fresh[t * 32 : (t + 1) * 32]
                sel_s[s // 4, rows, lanes] = sel[t * 32 : (t + 1) * 32, lanes]
        sum_s[axis] = total

    for s in range(16):
        step_t[s] = step_s[s].T
        fresh_t[s] = fresh_s[s].T
        if s % 4 == 0:
            sel_t[s * 32 : s * 32 + 128, :] = sel_s[s // 4].T

    def group(g, carry):
        rows = pl.ds(pl.multiple_of(g * 8, 8), 8)
        rates = [rate_far[n, rows, :] for n in range(N)]
        state = None
        for s in range(16):
            step = step_t[s, rows, :]
            fresh = fresh_t[s, rows, :]
            following = []
            total = [None, None]
            for n in range(N):
                at = s * 32 + n
                new = fresh * sel_t[at : at + 1, :]
                if state is not None:
                    new = new + jnp.exp2(step * rates[n]) * state[n]
                following.append(new)
                term = new * sel_t[at + N : at + N + 1, :]
                total[n % 2] = term if total[n % 2] is None else total[n % 2] + term
            state = following
            y_s[s, rows, :] = total[0] + total[1]
        return carry

    lax.fori_loop(0, 16, group, 0)
    turned = [y_s[s].T for s in range(16)]
    sums = []
    for axis in range(2):
        rows = []
        for t in range(16):
            both = turned[t][axis * 64 : axis * 64 + 32] + turned[15 - t][axis * 64 + 32 : axis * 64 + 64]
            rows.append(sum_s[axis, t * 32 : (t + 1) * 32, :] + both * LN2)
        sums.append(rows)
    halves = [jnp.concatenate([row[h * 16 : (h + 1) * 16] for row in sums[0]], axis=0).astype(BF16) for h in range(2)]
    along_y = jnp.dot(swap[...], jnp.concatenate(halves, axis=1), preferred_element_type=F32)
    hidden = []
    for h in range(2):
        along_x = jnp.concatenate([row[h * 16 : (h + 1) * 16] for row in sums[1]], axis=0)
        hidden.append((along_y[:, h * E : (h + 1) * E] + along_x) * gate_s[h])
    out[...] = leave(hidden[0], hidden[1], w_out[...]).astype(BF16)


def z_softplus(x):
    tail = jnp.exp2(jnp.abs(x) * (-LOG2E))
    return jnp.maximum(x, 0.0) + jnp.where(tail < 1e-4, tail, jnp.log(1.0 + tail))


def normalise(values, gain2, plain, rolled):
    low = iota(values.shape, 1) < C
    squares = values * values
    first = jnp.sum(jnp.where(low, squares, 0.0), axis=1, keepdims=True) * (1.0 / C)
    second = jnp.sum(jnp.where(low, 0.0, squares), axis=1, keepdims=True) * (1.0 / C)
    scale = jnp.where(low, lax.rsqrt(first + 1e-05), lax.rsqrt(second + 1e-05))
    normed = (values * scale * gain2).astype(BF16).astype(F32)
    plain[...] = normed
    rolled[...] = pltpu.roll(normed, C, 1)


def project(blocks, lhsq):
    half = jnp.concatenate(blocks, axis=0)
    zero = jnp.zeros_like(half)
    rows = jnp.concatenate(
        [jnp.concatenate([half, zero], axis=1), jnp.concatenate([zero, half], axis=1)], axis=0
    ).astype(BF16)
    both = lax.dot_general(lhsq, rows, NT, preferred_element_type=F32)
    return both[:EQ].astype(BF16).astype(F32), both[EQ:]


def z_step(d, index, neighbours, table, xp, quarter, act_s, sel_s, step_s, fresh_s):
    pre = table[index, CB0]
    for k in range(K):
        if neighbours[k] is not None:
            pre = pre + table[index, CW0 + k] * neighbours[k]
    act = silu(pre).astype(BF16).astype(F32)
    spread = jnp.concatenate([jnp.where(quarter == q, act, 0.0) for q in range(Q)], axis=0).astype(BF16)
    sel = jnp.dot(xp[index], spread, preferred_element_type=F32)
    sel = sel + pltpu.roll(sel, 64, 1)
    sel = sel + pltpu.roll(sel, 32, 1)
    raw = table[index, DB0]
    for r in range(R):
        raw = raw + table[index, DW0 + r] * sel[2 * N + r : 2 * N + r + 1, :]
    step = z_softplus(raw)
    return act, sel, step


def scan_group(index, d, rows, start, table, sel_s, step_s, fresh_s, y_s):
    rates = [table[index, A0 + n, rows, :] for n in range(N)]
    state = start
    for s in range(STEPS):
        t = s if d == 0 else STEPS - 1 - s
        step = step_s[d, t, rows, :]
        fresh = fresh_s[d, t, rows, :]
        total = [None, None]
        following = []
        for n in range(N):
            new = fresh * sel_s[d, t, n : n + 1, :]
            if state is not None:
                new = new + jnp.exp2(step * rates[n]) * state[n]
            following.append(new)
            term = new * sel_s[d, t, N + n : N + n + 1, :]
            total[n % 2] = term if total[n % 2] is None else total[n % 2] + term
        state = following
        y_s[t, rows, :] = y_s[t, rows, :] + (total[0] + total[1])
    return state


def gated_rows(y_s, gate_s, turned_s):
    for t in range(STEPS):
        turned_s[t] = (y_s[t] * gate_s[t]).T


def line_inputs_kernel(values, table, lhsq_ref, xp, gain2, gate_s, sel_s, step_s, fresh_s, y_s, plain, rolled, inner_s):
    normalise(values[...].astype(F32), gain2[...], plain, rolled)
    lane = iota((EQ, E), 1)
    quarter = lane // LINES
    chunk = lane % STEPS
    low = iota((STEPS, 2 * C), 1) < C
    lhsq = lhsq_ref[...]
    for t in range(STEPS):
        blocks = []
        for half in range(2):
            for y in range(2):
                where = pl.ds(y * 128 + t // 2, STEPS, stride=8)
                rows = plain[where, :] if t % 2 == half else rolled[where, :]
                blocks.append(jnp.where(low, rows, 0.0) if half == 0 else jnp.where(low, 0.0, rows))
        inner, gate = project(blocks, lhsq)
        inner_s[t] = inner
        gate_s[t] = silu(gate)
    for d in range(2):
        edge = (chunk >= 1) if d == 0 else (chunk < STEPS - 1)
        for t in range(STEPS):
            near = []
            for k in range(K):
                p = t - 3 + k if d == 0 else t + 3 - k
                if 0 <= p < STEPS:
                    near.append(inner_s[p])
                else:
                    moved = pltpu.roll(inner_s[p % STEPS], 1 if d == 0 else E - 1, 1)
                    near.append(jnp.where(edge, moved, 0.0))
            act, sel, step = z_step(d, d, near, table, xp, quarter, None, sel_s, step_s, fresh_s)
            sel_s[d, t] = sel
            step_s[d, t] = step
            fresh_s[d, t] = step * act
            direct = table[d, SK0] * act
            y_s[t] = direct if d == 0 else y_s[t] + direct


def line_scan_kernel(table, wo, gate_s, sel_s, step_s, fresh_s, direct_s, out, y_s, turned_s):
    far_off = 1e4
    y_s[...] = direct_s[...]

    def group(g, carry):
        rows = pl.ds(pl.multiple_of(g * 8, 8), 8)
        place = iota((8, E), 1) % STEPS
        for d in range(2):
            rates = [table[d, A0 + n, rows, :] for n in range(N)]
            ends = None
            whole = None
            for s in range(STEPS):
                t = s if d == 0 else STEPS - 1 - s
                step = step_s[d, t, rows, :]
                fresh = fresh_s[d, t, rows, :]
                whole = step if whole is None else whole + step
                following = []
                for n in range(N):
                    new = fresh * sel_s[d, t, n : n + 1, :]
                    if ends is not None:
                        new = new + jnp.exp2(step * rates[n]) * ends[n]
                    following.append(new)
                ends = following
            before = place if d == 0 else STEPS - 1 - place

            def moved(x, k, d=d):
                return pltpu.roll(x, k if d == 0 else E - k, 1)

            def kept(k, x, before=before):
                return jnp.where(before >= k, x, far_off)

            one = moved(whole, 1)
            two = one + moved(whole, 2)
            three = two + moved(whole, 3)
            four = three + moved(whole, 4)
            eight = four + moved(four, 4)
            twelve = eight + moved(four, 8)
            spans = [kept(2, one), kept(3, two), kept(4, three)]
            wide = [kept(4, four), kept(8, eight), kept(12, twelve)]
            start = []
            for n in range(N):
                sums = jnp.where(before >= 1, moved(ends[n], 1), 0.0)
                for k in range(3):
                    sums = sums + jnp.exp2(spans[k] * rates[n]) * moved(ends[n], k + 2)
                start.append(sums)
            for n in range(N):
                sums = start[n]
                for k in range(3):
                    sums = sums + jnp.exp2(wide[k] * rates[n]) * moved(start[n], 4 * k + 4)
                start[n] = sums
            scan_group(d, d, rows, start, table, sel_s, step_s, fresh_s, y_s)
        return carry

    lax.fori_loop(0, EQ // 8, group, 0)
    gated_rows(y_s, gate_s, turned_s)
    near = None
    for q in range(Q):
        for half in range(2):
            steps = [turned_s[2 * p + half, q * LINES : (q + 1) * LINES, :] for p in range(8)]
            lhs = jnp.concatenate(steps, axis=0).astype(BF16)
            part = jnp.dot(lhs, wo[q, half], preferred_element_type=F32)
            near = part if near is None else near + part
    for p in range(8):
        for y in range(2):
            first = p * LINES + y * STEPS
            out[pl.ds(2 * p + y, STEPS, stride=16), :] = near[first : first + STEPS]


def vmem(count):
    return [pl.BlockSpec(memory_space=pltpu.VMEM)] * count


def prepare(*weights):
    shapes = [
        jax.ShapeDtypeStruct((6, VEC, E), F32),
        jax.ShapeDtypeStruct((N, E, E), F32),
        jax.ShapeDtypeStruct((6, 2 * E, 2 * E), BF16),
        jax.ShapeDtypeStruct((2 * C, 4 * E), BF16),
        jax.ShapeDtypeStruct((2 * E, 2 * C), BF16),
        jax.ShapeDtypeStruct((1, 2 * C), F32),
        jax.ShapeDtypeStruct((256, 256), BF16),
        jax.ShapeDtypeStruct((2, ROWS, EQ, E), F32),
        jax.ShapeDtypeStruct((2 * EQ, Q * C), BF16),
        jax.ShapeDtypeStruct((2, 40, E), BF16),
        jax.ShapeDtypeStruct((Q, 2, EQ, 2 * C), BF16),
    ]
    ready = pl.pallas_call(
        prepare_kernel,
        out_shape=shapes,
        in_specs=[pl.BlockSpec(memory_space=pl.ANY)] * 10,
        out_specs=vmem(11),
        scratch_shapes=[pltpu.VMEM(w.shape, w.dtype) for w in weights] + [pltpu.SemaphoreType.DMA((10,))],
        compiler_params=PARAMS,
        name="prepare",
    )(*[pltpu.with_memory_space_constraint(w, pltpu.HBM) for w in weights])
    return ready[:7], (*ready[7:], ready[5])


def planes(values, ready):
    return pl.pallas_call(
        plane_kernel,
        out_shape=jax.ShapeDtypeStruct((256, 2 * C), BF16),
        in_specs=vmem(8),
        out_specs=vmem(1)[0],
        scratch_shapes=[
            pltpu.VMEM((2, 704, E), F32),
            pltpu.VMEM((2, 256, E), F32),
            pltpu.VMEM((16, E, E), F32),
            pltpu.VMEM((16, E, E), F32),
            pltpu.VMEM((4, E, E), F32),
            pltpu.VMEM((16, E, E), F32),
            pltpu.VMEM((16, E, E), F32),
            pltpu.VMEM((16 * 2 * N, E), F32),
            pltpu.VMEM((16, E, E), F32),
            pltpu.VMEM((2, 512, E), F32),
        ],
        compiler_params=PARAMS,
        name="planes",
    )(values, *ready)


def z_inputs(values, ready):
    table, lhsq, xp, _, gain2 = ready
    return pl.pallas_call(
        line_inputs_kernel,
        out_shape=[
            jax.ShapeDtypeStruct((STEPS, EQ, E), F32),
            jax.ShapeDtypeStruct((2, STEPS, 40, E), F32),
            jax.ShapeDtypeStruct((2, STEPS, EQ, E), F32),
            jax.ShapeDtypeStruct((2, STEPS, EQ, E), F32),
            jax.ShapeDtypeStruct((STEPS, EQ, E), F32),
        ],
        in_specs=vmem(5),
        out_specs=vmem(5),
        scratch_shapes=[pltpu.VMEM((256, E), F32), pltpu.VMEM((256, E), F32), pltpu.VMEM((STEPS, EQ, E), F32)],
        compiler_params=PARAMS,
        name="z_inputs",
    )(values, table, lhsq, xp, gain2)


def z_lines(given, ready):
    table, _, _, wo, _ = ready
    return pl.pallas_call(
        line_scan_kernel,
        out_shape=jax.ShapeDtypeStruct((256, 2 * C), F32),
        in_specs=vmem(7),
        out_specs=vmem(1)[0],
        scratch_shapes=[pltpu.VMEM((STEPS, EQ, E), F32), pltpu.VMEM((STEPS, E, EQ), F32)],
        compiler_params=PARAMS,
        name="z_lines",
    )(table, wo, *given)


def local(voxels, norm_gain, in_weight, conv_weight, conv_bias, x_weight, dt_weight, dt_bias, a_rate, skip_gain, out_weight):
    pairs = voxels.reshape(2, 128, 2 * C)
    sent = pairs.transpose(1, 0, 2)
    arrived = lax.all_to_all(sent, ("row", "col"), split_axis=0, concat_axis=0, tiled=True)
    ready, z_ready = prepare(
        in_weight,
        conv_weight,
        conv_bias,
        x_weight.transpose(0, 2, 1),
        dt_weight,
        dt_bias,
        a_rate.transpose(0, 2, 1),
        skip_gain,
        out_weight.T,
        norm_gain.reshape(1, C),
    )
    given = z_inputs(pairs.reshape(256, 2 * C), z_ready)
    far = planes(arrived.reshape(256, 2 * C), ready)
    returned = lax.all_to_all(far.reshape(128, 2, 2 * C), ("row", "col"), split_axis=0, concat_axis=0, tiled=True)
    near = z_lines(given, z_ready)
    mixed = (near.reshape(128, 2, 2 * C) + returned.astype(F32)).astype(BF16)
    return mixed.transpose(1, 0, 2).reshape(1, 2, 128 * 2 * C)


def solution(mesh):
    in_specs = (P("row", "col", None),) + (P(),) * 10
    return jax.shard_map(local, mesh=mesh, in_specs=in_specs, out_specs=P("row", "col", None), check_vma=False)
```

```python
import math

import jax
import jax.numpy as jnp
from jax import lax
from jax.experimental import pallas as pl
from jax.experimental.pallas import tpu as pltpu
from jax.sharding import PartitionSpec as P

C = 64
E = 128
N = 16
R = 4
K = 4
PAD = 8
CW, CB, DB, SK, VEC = 0, 4, 5, 6, 8
Q = 4
EQ = E // Q
STEPS = 16
LINES = 32
A0, CW0, DW0, CB0, DB0, SK0, ROWS = 0, 16, 20, 24, 25, 26, 32
LN2 = math.log(2.0)
LOG2E = 1.0 / LN2
F32 = jnp.float32
BF16 = jnp.bfloat16
HIGHEST = lax.Precision.HIGHEST
NT = (((1,), (1,)), ((), ()))
TN = (((0,), (0,)), ((), ()))
PARAMS = pltpu.CompilerParams(vmem_limit_bytes=48 * 1024 * 1024)


def iota(shape, axis):
    return lax.broadcasted_iota(jnp.int32, shape, axis)


def silu(x):
    half = 0.5 * x
    return half * (1.0 + jnp.tanh(half))


def softplus2(x):
    tail = jnp.exp2(-jnp.abs(x))
    return jnp.maximum(x, 0.0) + jnp.where(tail < 1e-4, tail * LOG2E, jnp.log2(1.0 + tail))


def prepare_kernel(*refs):
    given, (vec, rate_far, w_step, w_in, w_out, gain2, swap), (table, lhsq, xp, wo) = refs[:10], refs[10:17], refs[17:21]
    here, sem = refs[21:31], refs[31]
    copies = [pltpu.make_async_copy(a, b, sem.at[i]) for i, (a, b) in enumerate(zip(given, here))]
    for copy in copies:
        copy.start()
    for copy in copies:
        copy.wait()
    in_w, conv_w, conv_b, x_w, dt_w, dt_b, rate, skip, out_w, gain = here
    row, column = iota((R + 2 * N, E), 0), iota((R + 2 * N, E), 1)
    pick = (row == column % (2 * N) + R).astype(F32)
    for d in range(2, 6):
        vec[d, CW : CW + K] = conv_w[d] * 0.5
        vec[d, CB : CB + 1] = conv_b[d : d + 1, :] * 0.5
        vec[d, DB : DB + 1] = dt_b[d : d + 1, :] * LOG2E
        vec[d, SK : SK + 1] = skip[d : d + 1, :]
        vec[d, SK + 1 :] = jnp.zeros((1, E), F32)
        given_w = x_w[d].astype(F32)
        both = lax.dot_general(given_w[:R], dt_w[d] * LOG2E, TN, precision=HIGHEST, preferred_element_type=F32)
        high = both.astype(BF16)
        w_step[d, 0:E, 0:E] = high
        w_step[d, E:, 0:E] = (both - high.astype(F32)).astype(BF16)
        w_step[d, 0:E, E:] = lax.dot_general(given_w, pick, TN, preferred_element_type=F32).astype(BF16)
        w_step[d, E:, E:] = jnp.zeros((E, E), BF16)
    row, column = iota((256, 256), 0), iota((256, 256), 1)
    swap[...] = (column == row % 16 * 16 + row // 16).astype(BF16)
    turned = jnp.concatenate([-rate[2 + i] for i in range(4)], axis=0).T
    high = turned.astype(BF16)
    both = jnp.concatenate([high, (turned - high.astype(F32)).astype(BF16)], axis=1)
    row, column = iota((8 * N, E), 0), iota((8 * N, E), 1)
    for n in range(N):
        chosen = ((row % N == n) & (row // N % 4 == column // 32)).astype(BF16)
        rate_far[n] = jnp.dot(both, chosen, preferred_element_type=F32)
    weight = in_w[...]
    zero = jnp.zeros((C, E), BF16)
    inner, gate = weight[:, :E], weight[:, E:]
    w_in[0:C] = jnp.concatenate([inner, zero, gate, zero], axis=1)
    w_in[C:] = jnp.concatenate([zero, inner, zero, gate], axis=1)
    turned = out_w[...].astype(F32)
    wide = jnp.concatenate([turned, turned], axis=0).T
    low_half = iota((E, 2 * C), 1) < C
    w_out[0:E] = jnp.where(low_half, wide, 0.0).astype(BF16)
    w_out[E:] = jnp.where(low_half, 0.0, wide).astype(BF16)
    gain2[...] = jnp.concatenate([gain[...], gain[...]], axis=1)
    mask = ((iota((EQ, E), 1) % EQ) == iota((EQ, E), 0)).astype(BF16)
    same = (iota((2 * E, E), 0) % E // EQ == iota((2 * E, E), 1) // EQ).astype(BF16)
    row, column = iota((40, 36), 0), iota((40, 36), 1)
    pick = (column == jnp.where(row < 2 * N, row + R, row - 2 * N)) & (row < 2 * N + R)
    pick = pick.astype(BF16)
    for d in range(2):
        rows = jnp.concatenate(
            [
                rate[d] * (-LOG2E),
                conv_w[d],
                dt_w[d],
                conv_b[d : d + 1, :],
                dt_b[d : d + 1, :],
                skip[d : d + 1, :],
                jnp.zeros((5, E), F32),
            ],
            axis=0,
        )
        high = rows.astype(BF16)
        rest = (rows - high.astype(F32)).astype(BF16)
        spread = jnp.concatenate(
            [(part[:, None, :] * mask[None]).reshape(ROWS * EQ, E) for part in (high, rest)], axis=1
        )
        table[d] = jnp.dot(spread, same, preferred_element_type=F32).reshape(ROWS, EQ, E)
        xp[d] = jnp.dot(pick, x_w[d], preferred_element_type=F32).astype(BF16)
    turned = in_w[...].astype(F32).T
    for part in range(2):
        blocks = [turned[part * E + q * EQ : part * E + (q + 1) * EQ] for q in range(Q)]
        lhsq[part * EQ : (part + 1) * EQ, :] = jnp.concatenate(blocks, axis=1).astype(BF16)
    for q in range(Q):
        for half in range(2):
            wo[q, half] = w_out[half * E + q * EQ : half * E + (q + 1) * EQ, :]


def enter(values, gain2):
    squares = values * values
    high = squares.astype(BF16)
    rest = (squares - high.astype(F32)).astype(BF16)
    block = iota((4 * C, 2 * C), 0) % (2 * C) // C == iota((4 * C, 2 * C), 1) // C
    total = jnp.dot(jnp.concatenate([high, rest], axis=1), block.astype(BF16), preferred_element_type=F32)
    return (values * lax.rsqrt(total * (1.0 / C) + 1e-05) * gain2).astype(BF16)


def leave(first, second, w_out):
    hidden = jnp.concatenate([first.astype(BF16), second.astype(BF16)], axis=1)
    return jnp.dot(hidden, w_out, preferred_element_type=F32)


def step_inputs(taps, vec, w_step):
    half = vec[CB : CB + 1, :]
    for k in range(K):
        half = half + vec[CW + k : CW + k + 1, :] * taps[k]
    act = (half + half * jnp.tanh(half)).astype(BF16)
    both = jnp.dot(jnp.concatenate([act, act], axis=1), w_step, preferred_element_type=F32)
    return act.astype(F32), softplus2(both[:, :E] + vec[DB : DB + 1, :]), both[:, E:]


def tree_sum(terms):
    while len(terms) > 1:
        terms = [terms[i] + terms[i + 1] for i in range(0, len(terms), 2)]
    return terms[0]


def plane_kernel(values, vec, rate_far, w_step, w_in, w_out, gain2, swap, out, lines_s, normed_s, step_s, fresh_s, sel_s, step_t, fresh_t, sel_t, y_s, direct_s):
    normed = enter(values[...].astype(F32), gain2[...])
    normed_s[...] = normed
    both = jnp.dot(normed, w_in[:, : 2 * E], preferred_element_type=F32).astype(BF16)
    inner = [both[:, h * E : (h + 1) * E].astype(F32) for h in range(2)]
    swapped = jnp.dot(swap[...], both, preferred_element_type=F32)
    zero = jnp.zeros((96, E), F32)
    for axis in range(2):
        lines_s[axis, 0:96, :] = zero
        lines_s[axis, 608:704, :] = zero
    for h in range(2):
        for i in range(16):
            first = 96 + i * 32 + h * 16
            lines_s[1, first : first + 16, :] = inner[h][i * 16 : (i + 1) * 16]
            lines_s[0, first : first + 16, :] = swapped[i * 16 : (i + 1) * 16, h * E : (h + 1) * E]

    for part in range(4):
        for axis in range(2):
            for d in range(2):
                index = 2 + 2 * axis + d
                begin = 4 * part if d == 0 else 12 - 4 * part
                firsts = [32 * (begin + (k if d == 0 else 6 - k)) for k in range(K)]
                taps = [lines_s[axis, first : first + 128, :] for first in firsts]
                act, step, sel = step_inputs(taps, vec[index], w_step[index])
                direct_s[axis, d, begin * 32 : begin * 32 + 128, :] = vec[index, SK : SK + 1, :] * act
                fresh = step * act
                rows = slice(axis * 64 + d * 32, axis * 64 + d * 32 + 32)
                for i in range(4):
                    t = i if d == 0 else 3 - i
                    lanes = slice(i * 32, i * 32 + 32)
                    step_s[4 * part + i, rows, :] = step[t * 32 : (t + 1) * 32]
                    fresh_s[4 * part + i, rows, :] = fresh[t * 32 : (t + 1) * 32]
                    sel_s[part, rows, lanes] = sel[t * 32 : (t + 1) * 32, lanes]
        for s in range(4 * part, 4 * part + 4):
            step_t[s] = step_s[s].T
            fresh_t[s] = fresh_s[s].T
        sel_t[part * 128 : part * 128 + 128, :] = sel_s[part].T

    def group(g, carry):
        rows = [pl.ds(pl.multiple_of(g * 16 + 8 * i, 8), 8) for i in range(2)]
        results = []
        for i in range(2):
            rates = [rate_far[n, rows[i], :] for n in range(N)]
            state = None
            result = []
            for s in range(16):
                step = step_t[s, rows[i], :]
                fresh = fresh_t[s, rows[i], :]
                following = []
                total = [None, None]
                for n in range(N):
                    at = s * 32 + n
                    new = fresh * sel_t[at : at + 1, :]
                    if state is not None:
                        new = new + jnp.exp2(step * rates[n]) * state[n]
                    following.append(new)
                    term = new * sel_t[at + N : at + N + 1, :]
                    total[n % 2] = term if total[n % 2] is None else total[n % 2] + term
                state = following
                result.append(total[0] + total[1])
            results.append(result)
        here = pl.ds(pl.multiple_of(g * 16, 16), 16)
        for s in range(16):
            y_s[s, here, :] = jnp.concatenate([results[0][s], results[1][s]], axis=0).astype(BF16)
        return carry

    lax.fori_loop(0, 8, group, 0)
    gates = silu(jnp.dot(normed_s[...], w_in[:, 2 * E :], preferred_element_type=F32))
    turned = [y_s[s].T.astype(F32) for s in range(16)]
    sums = []
    for axis in range(2):
        rows = []
        for t in range(16):
            both = turned[t][axis * 64 : axis * 64 + 32] + turned[15 - t][axis * 64 + 32 : axis * 64 + 64]
            here = pl.ds(t * 32, 32)
            rows.append(direct_s[axis, 0, here, :] + direct_s[axis, 1, here, :] + both * LN2)
        sums.append(rows)
    halves = [jnp.concatenate([row[h * 16 : (h + 1) * 16] for row in sums[0]], axis=0).astype(BF16) for h in range(2)]
    along_y = jnp.dot(swap[...], jnp.concatenate(halves, axis=1), preferred_element_type=F32)
    hidden = []
    for h in range(2):
        along_x = jnp.concatenate([row[h * 16 : (h + 1) * 16] for row in sums[1]], axis=0)
        hidden.append((along_y[:, h * E : (h + 1) * E] + along_x) * gates[:, h * E : (h + 1) * E])
    out[...] = leave(hidden[0], hidden[1], w_out[...]).astype(BF16)


def z_softplus(x):
    tail = jnp.exp2(jnp.abs(x) * (-LOG2E))
    return jnp.maximum(x, 0.0) + jnp.where(tail < 1e-4, tail, jnp.log(1.0 + tail))


def normalise(values, gain2, plain, rolled):
    low = iota(values.shape, 1) < C
    squares = values * values
    first = jnp.sum(jnp.where(low, squares, 0.0), axis=1, keepdims=True) * (1.0 / C)
    second = jnp.sum(jnp.where(low, 0.0, squares), axis=1, keepdims=True) * (1.0 / C)
    scale = jnp.where(low, lax.rsqrt(first + 1e-05), lax.rsqrt(second + 1e-05))
    normed = (values * scale * gain2).astype(BF16).astype(F32)
    plain[...] = normed
    rolled[...] = pltpu.roll(normed, C, 1)


def project(blocks, lhsq):
    half = jnp.concatenate(blocks, axis=0)
    zero = jnp.zeros_like(half)
    rows = jnp.concatenate(
        [jnp.concatenate([half, zero], axis=1), jnp.concatenate([zero, half], axis=1)], axis=0
    ).astype(BF16)
    both = lax.dot_general(lhsq, rows, NT, preferred_element_type=F32)
    return both[:EQ].astype(BF16).astype(F32), both[EQ:]


def z_step(d, index, neighbours, table, xp, quarter, act_s, sel_s, step_s, fresh_s):
    pre = table[index, CB0]
    for k in range(K):
        if neighbours[k] is not None:
            pre = pre + table[index, CW0 + k] * neighbours[k]
    act = silu(pre).astype(BF16).astype(F32)
    spread = jnp.concatenate([jnp.where(quarter == q, act, 0.0) for q in range(Q)], axis=0).astype(BF16)
    sel = jnp.dot(xp[index], spread, preferred_element_type=F32)
    sel = sel + pltpu.roll(sel, 64, 1)
    sel = sel + pltpu.roll(sel, 32, 1)
    raw = table[index, DB0]
    for r in range(R):
        raw = raw + table[index, DW0 + r] * sel[2 * N + r : 2 * N + r + 1, :]
    step = z_softplus(raw)
    return act, sel, step


def scan_group(index, d, rows, start, table, sel_s, step_s, fresh_s, y_s):
    rates = [table[index, A0 + n, rows, :] for n in range(N)]
    state = start
    for s in range(STEPS):
        t = s if d == 0 else STEPS - 1 - s
        step = step_s[d, t, rows, :]
        fresh = fresh_s[d, t, rows, :]
        total = [None, None]
        following = []
        for n in range(N):
            new = fresh * sel_s[d, t, n : n + 1, :]
            if state is not None:
                new = new + jnp.exp2(step * rates[n]) * state[n]
            following.append(new)
            term = new * sel_s[d, t, N + n : N + n + 1, :]
            total[n % 2] = term if total[n % 2] is None else total[n % 2] + term
        state = following
        y_s[t, rows, :] = y_s[t, rows, :] + (total[0] + total[1])
    return state


def gated_rows(y_s, gate_s, turned_s):
    for t in range(STEPS):
        turned_s[t] = (y_s[t] * gate_s[t]).T


def line_inputs_kernel(values, table, lhsq_ref, xp, gain2, gate_s, sel_s, step_s, fresh_s, y_s, plain, rolled, inner_s):
    normalise(values[...].astype(F32), gain2[...], plain, rolled)
    lane = iota((EQ, E), 1)
    quarter = lane // LINES
    chunk = lane % STEPS
    low = iota((STEPS, 2 * C), 1) < C
    lhsq = lhsq_ref[...]
    for t in range(STEPS):
        blocks = []
        for half in range(2):
            for y in range(2):
                where = pl.ds(y * 128 + t // 2, STEPS, stride=8)
                rows = plain[where, :] if t % 2 == half else rolled[where, :]
                blocks.append(jnp.where(low, rows, 0.0) if half == 0 else jnp.where(low, 0.0, rows))
        inner, gate = project(blocks, lhsq)
        inner_s[t] = inner
        gate_s[t] = silu(gate)
    for d in range(2):
        edge = (chunk >= 1) if d == 0 else (chunk < STEPS - 1)
        for t in range(STEPS):
            near = []
            for k in range(K):
                p = t - 3 + k if d == 0 else t + 3 - k
                if 0 <= p < STEPS:
                    near.append(inner_s[p])
                else:
                    moved = pltpu.roll(inner_s[p % STEPS], 1 if d == 0 else E - 1, 1)
                    near.append(jnp.where(edge, moved, 0.0))
            act, sel, step = z_step(d, d, near, table, xp, quarter, None, sel_s, step_s, fresh_s)
            sel_s[d, t] = sel
            step_s[d, t] = step
            fresh_s[d, t] = step * act
            direct = table[d, SK0] * act
            y_s[t] = direct if d == 0 else y_s[t] + direct


def line_scan_kernel(table, wo, gate_s, sel_s, step_s, fresh_s, direct_s, out, y_s, turned_s):
    far_off = 1e4
    y_s[...] = direct_s[...]

    def group(g, carry):
        rows = pl.ds(pl.multiple_of(g * 8, 8), 8)
        place = iota((8, E), 1) % STEPS
        for d in range(2):
            rates = [table[d, A0 + n, rows, :] for n in range(N)]
            ends = None
            whole = None
            for s in range(STEPS):
                t = s if d == 0 else STEPS - 1 - s
                step = step_s[d, t, rows, :]
                fresh = fresh_s[d, t, rows, :]
                whole = step if whole is None else whole + step
                following = []
                for n in range(N):
                    new = fresh * sel_s[d, t, n : n + 1, :]
                    if ends is not None:
                        new = new + jnp.exp2(step * rates[n]) * ends[n]
                    following.append(new)
                ends = following
            before = place if d == 0 else STEPS - 1 - place

            def moved(x, k, d=d):
                return pltpu.roll(x, k if d == 0 else E - k, 1)

            def kept(k, x, before=before):
                return jnp.where(before >= k, x, far_off)

            one = moved(whole, 1)
            two = one + moved(whole, 2)
            three = two + moved(whole, 3)
            four = three + moved(whole, 4)
            eight = four + moved(four, 4)
            twelve = eight + moved(four, 8)
            spans = [kept(2, one), kept(3, two), kept(4, three)]
            wide = [kept(4, four), kept(8, eight), kept(12, twelve)]
            start = []
            for n in range(N):
                sums = jnp.where(before >= 1, moved(ends[n], 1), 0.0)
                for k in range(3):
                    sums = sums + jnp.exp2(spans[k] * rates[n]) * moved(ends[n], k + 2)
                start.append(sums)
            for n in range(N):
                sums = start[n]
                for k in range(3):
                    sums = sums + jnp.exp2(wide[k] * rates[n]) * moved(start[n], 4 * k + 4)
                start[n] = sums
            scan_group(d, d, rows, start, table, sel_s, step_s, fresh_s, y_s)
        return carry

    lax.fori_loop(0, EQ // 8, group, 0)
    gated_rows(y_s, gate_s, turned_s)
    near = None
    for q in range(Q):
        for half in range(2):
            steps = [turned_s[2 * p + half, q * LINES : (q + 1) * LINES, :] for p in range(8)]
            lhs = jnp.concatenate(steps, axis=0).astype(BF16)
            part = jnp.dot(lhs, wo[q, half], preferred_element_type=F32)
            near = part if near is None else near + part
    for p in range(8):
        for y in range(2):
            first = p * LINES + y * STEPS
            out[pl.ds(2 * p + y, STEPS, stride=16), :] = near[first : first + STEPS]


def vmem(count):
    return [pl.BlockSpec(memory_space=pltpu.VMEM)] * count


def prepare(*weights):
    shapes = [
        jax.ShapeDtypeStruct((6, VEC, E), F32),
        jax.ShapeDtypeStruct((N, E, E), F32),
        jax.ShapeDtypeStruct((6, 2 * E, 2 * E), BF16),
        jax.ShapeDtypeStruct((2 * C, 4 * E), BF16),
        jax.ShapeDtypeStruct((2 * E, 2 * C), BF16),
        jax.ShapeDtypeStruct((1, 2 * C), F32),
        jax.ShapeDtypeStruct((256, 256), BF16),
        jax.ShapeDtypeStruct((2, ROWS, EQ, E), F32),
        jax.ShapeDtypeStruct((2 * EQ, Q * C), BF16),
        jax.ShapeDtypeStruct((2, 40, E), BF16),
        jax.ShapeDtypeStruct((Q, 2, EQ, 2 * C), BF16),
    ]
    ready = pl.pallas_call(
        prepare_kernel,
        out_shape=shapes,
        in_specs=[pl.BlockSpec(memory_space=pl.ANY)] * 10,
        out_specs=vmem(11),
        scratch_shapes=[pltpu.VMEM(w.shape, w.dtype) for w in weights] + [pltpu.SemaphoreType.DMA((10,))],
        compiler_params=PARAMS,
        name="prepare",
    )(*[pltpu.with_memory_space_constraint(w, pltpu.HBM) for w in weights])
    return ready[:7], (*ready[7:], ready[5])


def planes(values, ready):
    return pl.pallas_call(
        plane_kernel,
        out_shape=jax.ShapeDtypeStruct((256, 2 * C), BF16),
        in_specs=vmem(8),
        out_specs=vmem(1)[0],
        scratch_shapes=[
            pltpu.VMEM((2, 704, E), F32),
            pltpu.VMEM((256, E), BF16),
            pltpu.VMEM((16, E, E), F32),
            pltpu.VMEM((16, E, E), F32),
            pltpu.VMEM((4, E, E), F32),
            pltpu.VMEM((16, E, E), F32),
            pltpu.VMEM((16, E, E), F32),
            pltpu.VMEM((16 * 2 * N, E), F32),
            pltpu.VMEM((16, E, E), BF16),
            pltpu.VMEM((2, 2, 512, E), F32),
        ],
        compiler_params=PARAMS,
        name="planes",
    )(values, *ready)


def z_inputs(values, ready):
    table, lhsq, xp, _, gain2 = ready
    return pl.pallas_call(
        line_inputs_kernel,
        out_shape=[
            jax.ShapeDtypeStruct((STEPS, EQ, E), F32),
            jax.ShapeDtypeStruct((2, STEPS, 40, E), F32),
            jax.ShapeDtypeStruct((2, STEPS, EQ, E), F32),
            jax.ShapeDtypeStruct((2, STEPS, EQ, E), F32),
            jax.ShapeDtypeStruct((STEPS, EQ, E), F32),
        ],
        in_specs=vmem(5),
        out_specs=vmem(5),
        scratch_shapes=[pltpu.VMEM((256, E), F32), pltpu.VMEM((256, E), F32), pltpu.VMEM((STEPS, EQ, E), F32)],
        compiler_params=PARAMS,
        name="z_inputs",
    )(values, table, lhsq, xp, gain2)


def z_lines(given, ready):
    table, _, _, wo, _ = ready
    return pl.pallas_call(
        line_scan_kernel,
        out_shape=jax.ShapeDtypeStruct((256, 2 * C), F32),
        in_specs=vmem(7),
        out_specs=vmem(1)[0],
        scratch_shapes=[pltpu.VMEM((STEPS, EQ, E), F32), pltpu.VMEM((STEPS, E, EQ), F32)],
        compiler_params=PARAMS,
        name="z_lines",
    )(table, wo, *given)


def local(voxels, norm_gain, in_weight, conv_weight, conv_bias, x_weight, dt_weight, dt_bias, a_rate, skip_gain, out_weight):
    pairs = voxels.reshape(2, 128, 2 * C)
    sent = pairs.transpose(1, 0, 2)
    arrived = lax.all_to_all(sent, ("row", "col"), split_axis=0, concat_axis=0, tiled=True)
    ready, z_ready = prepare(
        in_weight,
        conv_weight,
        conv_bias,
        x_weight.transpose(0, 2, 1),
        dt_weight,
        dt_bias,
        a_rate.transpose(0, 2, 1),
        skip_gain,
        out_weight.T,
        norm_gain.reshape(1, C),
    )
    given = z_inputs(pairs.reshape(256, 2 * C), z_ready)
    far = planes(arrived.reshape(256, 2 * C), ready)
    returned = lax.all_to_all(far.reshape(128, 2, 2 * C), ("row", "col"), split_axis=0, concat_axis=0, tiled=True)
    near = z_lines(given, z_ready)
    mixed = (near.reshape(128, 2, 2 * C) + returned.astype(F32)).astype(BF16)
    return mixed.transpose(1, 0, 2).reshape(1, 2, 128 * 2 * C)


def solution(mesh):
    in_specs = (P("row", "col", None),) + (P(),) * 10
    return jax.shard_map(local, mesh=mesh, in_specs=in_specs, out_specs=P("row", "col", None), check_vma=False)
```

```python
import math

import jax
import jax.numpy as jnp
from jax import lax
from jax.experimental import pallas as pl
from jax.experimental.pallas import tpu as pltpu
from jax.sharding import PartitionSpec as P

C = 64
E = 128
N = 16
R = 4
K = 4
PAD = 8
CW, CB, DB, SK, VEC = 0, 4, 5, 6, 8
Q = 4
EQ = E // Q
STEPS = 16
LINES = 32
A0, CW0, DW0, CB0, DB0, SK0, ROWS = 0, 16, 20, 24, 25, 26, 32
XW = 3
SEL = 48
LN2 = math.log(2.0)
LOG2E = 1.0 / LN2
F32 = jnp.float32
BF16 = jnp.bfloat16
HIGHEST = lax.Precision.HIGHEST
NT = (((1,), (1,)), ((), ()))
TN = (((0,), (0,)), ((), ()))
PARAMS = pltpu.CompilerParams(vmem_limit_bytes=48 * 1024 * 1024)


def iota(shape, axis):
    return lax.broadcasted_iota(jnp.int32, shape, axis)


def silu(x):
    half = 0.5 * x
    return half * (1.0 + jnp.tanh(half))


def softplus2(x):
    tail = jnp.exp2(-jnp.abs(x))
    return jnp.maximum(x, 0.0) + jnp.where(tail < 1e-4, tail * LOG2E, jnp.log2(1.0 + tail))


def prepare_kernel(*refs):
    given, (vec, rate_far, w_step, w_in, w_out, gain2, swap), (table, lhsq, xp, wo) = refs[:10], refs[10:17], refs[17:21]
    here, sem = refs[21:30], refs[30]
    names = [i for i in range(10) if i != XW]
    copies = [pltpu.make_async_copy(given[i], here[at], sem.at[at]) for at, i in enumerate(names)]
    for copy in copies:
        copy.start()
    for copy in copies:
        copy.wait()
    in_w, conv_w, conv_b, dt_w, dt_b, rate, skip, out_w, gain = here
    x_w = given[XW]
    row, column = iota((R + 2 * N, E), 0), iota((R + 2 * N, E), 1)
    pick = (row == column % (2 * N) + R).astype(F32)
    for d in range(2, 6):
        vec[d, CW : CW + K] = conv_w[d] * 0.5
        vec[d, CB : CB + 1] = conv_b[d : d + 1, :] * 0.5
        vec[d, DB : DB + 1] = dt_b[d : d + 1, :] * LOG2E
        vec[d, SK : SK + 1] = skip[d : d + 1, :]
        vec[d, SK + 1 :] = jnp.zeros((1, E), F32)
        given_w = x_w[d].astype(F32)
        both = lax.dot_general(given_w[:R], dt_w[d] * LOG2E, TN, precision=HIGHEST, preferred_element_type=F32)
        high = both.astype(BF16)
        w_step[d, 0:E, 0:E] = high
        w_step[d, E:, 0:E] = (both - high.astype(F32)).astype(BF16)
        w_step[d, 0:E, E:] = lax.dot_general(given_w, pick, TN, preferred_element_type=F32).astype(BF16)
        w_step[d, E:, E:] = jnp.zeros((E, E), BF16)
    row, column = iota((256, 256), 0), iota((256, 256), 1)
    swap[...] = (column == row % 16 * 16 + row // 16).astype(BF16)
    turned = jnp.concatenate([-rate[2 + i] for i in range(4)], axis=0).T
    high = turned.astype(BF16)
    both = jnp.concatenate([high, (turned - high.astype(F32)).astype(BF16)], axis=1)
    row, column = iota((8 * N, E), 0), iota((8 * N, E), 1)
    for n in range(N):
        chosen = ((row % N == n) & (row // N % 4 == column // 32)).astype(BF16)
        rate_far[n] = jnp.dot(both, chosen, preferred_element_type=F32)
    weight = in_w[...]
    zero = jnp.zeros((C, E), BF16)
    inner, gate = weight[:, :E], weight[:, E:]
    w_in[0:C] = jnp.concatenate([inner, zero, gate, zero], axis=1)
    w_in[C:] = jnp.concatenate([zero, inner, zero, gate], axis=1)
    turned = out_w[...].astype(F32)
    wide = jnp.concatenate([turned, turned], axis=0).T
    low_half = iota((E, 2 * C), 1) < C
    w_out[0:E] = jnp.where(low_half, wide, 0.0).astype(BF16)
    w_out[E:] = jnp.where(low_half, 0.0, wide).astype(BF16)
    gain2[...] = jnp.concatenate([gain[...], gain[...]], axis=1)
    mask = ((iota((EQ, E), 1) % EQ) == iota((EQ, E), 0)).astype(BF16)
    same = (iota((2 * E, E), 0) % E // EQ == iota((2 * E, E), 1) // EQ).astype(BF16)
    row, column = iota((SEL, 36), 0), iota((SEL, 36), 1)
    pick = (column == jnp.where(row < 2 * N, row + R, row - 2 * N)) & (row < 2 * N + R)
    pick = pick.astype(BF16)
    for d in range(2):
        rows = jnp.concatenate(
            [
                rate[d] * (-LOG2E),
                conv_w[d],
                dt_w[d],
                conv_b[d : d + 1, :],
                dt_b[d : d + 1, :],
                skip[d : d + 1, :],
                jnp.zeros((5, E), F32),
            ],
            axis=0,
        )
        high = rows.astype(BF16)
        rest = (rows - high.astype(F32)).astype(BF16)
        spread = jnp.concatenate(
            [(part[:, None, :] * mask[None]).reshape(ROWS * EQ, E) for part in (high, rest)], axis=1
        )
        table[d] = jnp.dot(spread, same, preferred_element_type=F32).reshape(ROWS, EQ, E)
        xp[d] = jnp.dot(pick, x_w[d], preferred_element_type=F32).astype(BF16)
    turned = in_w[...].astype(F32).T
    for part in range(2):
        blocks = [turned[part * E + q * EQ : part * E + (q + 1) * EQ] for q in range(Q)]
        lhsq[part * EQ : (part + 1) * EQ, :] = jnp.concatenate(blocks, axis=1).astype(BF16)
    for q in range(Q):
        for half in range(2):
            wo[q, half] = w_out[half * E + q * EQ : half * E + (q + 1) * EQ, :]


def enter(values, gain2):
    squares = values * values
    high = squares.astype(BF16)
    rest = (squares - high.astype(F32)).astype(BF16)
    block = iota((4 * C, 2 * C), 0) % (2 * C) // C == iota((4 * C, 2 * C), 1) // C
    total = jnp.dot(jnp.concatenate([high, rest], axis=1), block.astype(BF16), preferred_element_type=F32)
    return (values * lax.rsqrt(total * (1.0 / C) + 1e-05) * gain2).astype(BF16)


def leave(first, second, w_out):
    hidden = jnp.concatenate([first.astype(BF16), second.astype(BF16)], axis=1)
    return jnp.dot(hidden, w_out, preferred_element_type=F32)


def step_inputs(taps, vec, w_step):
    half = vec[CB : CB + 1, :]
    for k in range(K):
        half = half + vec[CW + k : CW + k + 1, :] * taps[k]
    act = (half + half * jnp.tanh(half)).astype(BF16)
    both = jnp.dot(jnp.concatenate([act, act], axis=1), w_step, preferred_element_type=F32)
    return act, softplus2(both[:, :E] + vec[DB : DB + 1, :]), both[:, E:]


def tree_sum(terms):
    while len(terms) > 1:
        terms = [terms[i] + terms[i + 1] for i in range(0, len(terms), 2)]
    return terms[0]


def plane_kernel(values, vec, rate_far, w_step, w_in, w_out, gain2, swap, out, lines_s, normed_s, step_s, act_s, sel_s, step_t, fresh_t, sel_t, y_s, direct_s):
    normed = enter(values[...].astype(F32), gain2[...])
    normed_s[...] = normed
    both = jnp.dot(normed, w_in[:, : 2 * E], preferred_element_type=F32).astype(BF16)
    inner = [both[:, h * E : (h + 1) * E].astype(F32) for h in range(2)]
    swapped = jnp.dot(swap[...], both, preferred_element_type=F32)
    zero = jnp.zeros((96, E), F32)
    for axis in range(2):
        lines_s[axis, 0:96, :] = zero
        lines_s[axis, 608:704, :] = zero
    for h in range(2):
        for i in range(16):
            first = 96 + i * 32 + h * 16
            lines_s[1, first : first + 16, :] = inner[h][i * 16 : (i + 1) * 16]
            lines_s[0, first : first + 16, :] = swapped[i * 16 : (i + 1) * 16, h * E : (h + 1) * E]

    for part in range(4):
        for axis in range(2):
            for d in range(2):
                index = 2 + 2 * axis + d
                begin = 4 * part if d == 0 else 12 - 4 * part
                firsts = [32 * (begin + (k if d == 0 else 6 - k)) for k in range(K)]
                taps = [lines_s[axis, first : first + 128, :] for first in firsts]
                act, step, sel = step_inputs(taps, vec[index], w_step[index])
                direct_s[axis, d, begin * 32 : begin * 32 + 128, :] = vec[index, SK : SK + 1, :] * act.astype(F32)
                rows = slice(axis * 64 + d * 32, axis * 64 + d * 32 + 32)
                for i in range(4):
                    t = i if d == 0 else 3 - i
                    lanes = slice(i * 32, i * 32 + 32)
                    step_s[4 * part + i, rows, :] = step[t * 32 : (t + 1) * 32]
                    act_s[4 * part + i, rows, :] = act[t * 32 : (t + 1) * 32]
                    sel_s[part, rows, lanes] = sel[t * 32 : (t + 1) * 32, lanes]
        for s in range(4 * part, 4 * part + 4):
            step = step_s[s].T
            step_t[s] = step
            fresh_t[s] = step * act_s[s].T.astype(F32)
        sel_t[part * 128 : part * 128 + 128, :] = sel_s[part].T

    def group(g, carry):
        rows = [pl.ds(pl.multiple_of(g * 16 + 8 * i, 8), 8) for i in range(2)]
        results = []
        for i in range(2):
            rates = [rate_far[n, rows[i], :] for n in range(N)]
            state = None
            result = []
            for s in range(16):
                step = step_t[s, rows[i], :]
                fresh = fresh_t[s, rows[i], :]
                following = []
                total = [None, None]
                for n in range(N):
                    at = s * 32 + n
                    new = fresh * sel_t[at : at + 1, :]
                    if state is not None:
                        new = new + jnp.exp2(step * rates[n]) * state[n]
                    following.append(new)
                    term = new * sel_t[at + N : at + N + 1, :]
                    total[n % 2] = term if total[n % 2] is None else total[n % 2] + term
                state = following
                result.append(total[0] + total[1])
            results.append(result)
        here = pl.ds(pl.multiple_of(g * 16, 16), 16)
        for s in range(16):
            y_s[s, here, :] = jnp.concatenate([results[0][s], results[1][s]], axis=0).astype(BF16)
        return carry

    lax.fori_loop(0, 8, group, 0)
    gates = silu(jnp.dot(normed_s[...], w_in[:, 2 * E :], preferred_element_type=F32))
    turned = [y_s[s].T.astype(F32) for s in range(16)]
    sums = []
    for axis in range(2):
        rows = []
        for t in range(16):
            both = turned[t][axis * 64 : axis * 64 + 32] + turned[15 - t][axis * 64 + 32 : axis * 64 + 64]
            here = pl.ds(t * 32, 32)
            rows.append(direct_s[axis, 0, here, :] + direct_s[axis, 1, here, :] + both * LN2)
        sums.append(rows)
    halves = [jnp.concatenate([row[h * 16 : (h + 1) * 16] for row in sums[0]], axis=0).astype(BF16) for h in range(2)]
    along_y = jnp.dot(swap[...], jnp.concatenate(halves, axis=1), preferred_element_type=F32)
    hidden = []
    for h in range(2):
        along_x = jnp.concatenate([row[h * 16 : (h + 1) * 16] for row in sums[1]], axis=0)
        hidden.append((along_y[:, h * E : (h + 1) * E] + along_x) * gates[:, h * E : (h + 1) * E])
    out[...] = leave(hidden[0], hidden[1], w_out[...]).astype(BF16)


def z_softplus(x):
    tail = jnp.exp2(jnp.abs(x) * (-LOG2E))
    return jnp.maximum(x, 0.0) + jnp.where(tail < 1e-4, tail, jnp.log(1.0 + tail))


def normalise(values, gain2, plain, rolled):
    low = iota(values.shape, 1) < C
    squares = values * values
    first = jnp.sum(jnp.where(low, squares, 0.0), axis=1, keepdims=True) * (1.0 / C)
    second = jnp.sum(jnp.where(low, 0.0, squares), axis=1, keepdims=True) * (1.0 / C)
    scale = jnp.where(low, lax.rsqrt(first + 1e-05), lax.rsqrt(second + 1e-05))
    normed = (values * scale * gain2).astype(BF16).astype(F32)
    plain[...] = normed
    rolled[...] = pltpu.roll(normed, C, 1)


def project(blocks, lhsq):
    half = jnp.concatenate(blocks, axis=0)
    zero = jnp.zeros_like(half)
    rows = jnp.concatenate(
        [jnp.concatenate([half, zero], axis=1), jnp.concatenate([zero, half], axis=1)], axis=0
    ).astype(BF16)
    both = lax.dot_general(lhsq, rows, NT, preferred_element_type=F32)
    return both[:EQ].astype(BF16).astype(F32), both[EQ:]


def z_step(d, index, neighbours, table, xp, quarter, act_s, sel_s, step_s, fresh_s):
    pre = table[index, CB0]
    for k in range(K):
        if neighbours[k] is not None:
            pre = pre + table[index, CW0 + k] * neighbours[k]
    act = silu(pre).astype(BF16).astype(F32)
    spread = jnp.concatenate([jnp.where(quarter == q, act, 0.0) for q in range(Q)], axis=0).astype(BF16)
    sel = jnp.dot(xp[index], spread, preferred_element_type=F32)
    sel = sel + pltpu.roll(sel, 64, 1)
    sel = sel + pltpu.roll(sel, 32, 1)
    raw = table[index, DB0]
    for r in range(R):
        raw = raw + table[index, DW0 + r] * sel[2 * N + r : 2 * N + r + 1, :]
    step = z_softplus(raw)
    return act, sel, step


def scan_group(index, d, rows, start, table, sel_s, step_s, fresh_s, y_s):
    rates = [table[index, A0 + n, rows, :] for n in range(N)]
    state = start
    for s in range(STEPS):
        t = s if d == 0 else STEPS - 1 - s
        step = step_s[d, t, rows, :]
        fresh = fresh_s[d, t, rows, :]
        total = [None, None]
        following = []
        for n in range(N):
            new = fresh * sel_s[d, t, n : n + 1, :]
            if state is not None:
                new = new + jnp.exp2(step * rates[n]) * state[n]
            following.append(new)
            term = new * sel_s[d, t, N + n : N + n + 1, :]
            total[n % 2] = term if total[n % 2] is None else total[n % 2] + term
        state = following
        y_s[t, rows, :] = y_s[t, rows, :] + (total[0] + total[1])
    return state


def gated_rows(y_s, gate_s, turned_s):
    for t in range(STEPS):
        turned_s[t] = (y_s[t] * gate_s[t]).T


def line_inputs_kernel(values, table, lhsq_ref, xp, gain2, gate_s, sel_s, step_s, fresh_s, y_s, plain, rolled, inner_s):
    normalise(values[...].astype(F32), gain2[...], plain, rolled)
    lane = iota((EQ, E), 1)
    quarter = lane // LINES
    chunk = lane % STEPS
    low = iota((STEPS, 2 * C), 1) < C
    lhsq = lhsq_ref[...]
    for t in range(STEPS):
        blocks = []
        for half in range(2):
            for y in range(2):
                where = pl.ds(y * 128 + t // 2, STEPS, stride=8)
                rows = plain[where, :] if t % 2 == half else rolled[where, :]
                blocks.append(jnp.where(low, rows, 0.0) if half == 0 else jnp.where(low, 0.0, rows))
        inner, gate = project(blocks, lhsq)
        inner_s[t] = inner
        gate_s[t] = silu(gate)
    for d in range(2):
        edge = (chunk >= 1) if d == 0 else (chunk < STEPS - 1)
        for t in range(STEPS):
            near = []
            for k in range(K):
                p = t - 3 + k if d == 0 else t + 3 - k
                if 0 <= p < STEPS:
                    near.append(inner_s[p])
                else:
                    moved = pltpu.roll(inner_s[p % STEPS], 1 if d == 0 else E - 1, 1)
                    near.append(jnp.where(edge, moved, 0.0))
            act, sel, step = z_step(d, d, near, table, xp, quarter, None, sel_s, step_s, fresh_s)
            sel_s[d, t] = sel
            step_s[d, t] = step
            fresh_s[d, t] = step * act
            direct = table[d, SK0] * act
            y_s[t] = direct if d == 0 else y_s[t] + direct


def line_scan_kernel(table, wo, gate_s, sel_s, step_s, fresh_s, direct_s, out, y_s, turned_s):
    far_off = 1e4
    y_s[...] = direct_s[...]

    def group(g, carry):
        rows = pl.ds(pl.multiple_of(g * 8, 8), 8)
        place = iota((8, E), 1) % STEPS
        for d in range(2):
            rates = [table[d, A0 + n, rows, :] for n in range(N)]
            ends = None
            whole = None
            for s in range(STEPS):
                t = s if d == 0 else STEPS - 1 - s
                step = step_s[d, t, rows, :]
                fresh = fresh_s[d, t, rows, :]
                whole = step if whole is None else whole + step
                following = []
                for n in range(N):
                    new = fresh * sel_s[d, t, n : n + 1, :]
                    if ends is not None:
                        new = new + jnp.exp2(step * rates[n]) * ends[n]
                    following.append(new)
                ends = following
            before = place if d == 0 else STEPS - 1 - place

            def moved(x, k, d=d):
                return pltpu.roll(x, k if d == 0 else E - k, 1)

            def kept(k, x, before=before):
                return jnp.where(before >= k, x, far_off)

            one = moved(whole, 1)
            two = one + moved(whole, 2)
            three = two + moved(whole, 3)
            four = three + moved(whole, 4)
            eight = four + moved(four, 4)
            twelve = eight + moved(four, 8)
            spans = [kept(2, one), kept(3, two), kept(4, three)]
            wide = [kept(4, four), kept(8, eight), kept(12, twelve)]
            start = []
            for n in range(N):
                sums = jnp.where(before >= 1, moved(ends[n], 1), 0.0)
                for k in range(3):
                    sums = sums + jnp.exp2(spans[k] * rates[n]) * moved(ends[n], k + 2)
                start.append(sums)
            for n in range(N):
                sums = start[n]
                for k in range(3):
                    sums = sums + jnp.exp2(wide[k] * rates[n]) * moved(start[n], 4 * k + 4)
                start[n] = sums
            scan_group(d, d, rows, start, table, sel_s, step_s, fresh_s, y_s)
        return carry

    lax.fori_loop(0, EQ // 8, group, 0)
    gated_rows(y_s, gate_s, turned_s)
    near = None
    for q in range(Q):
        for half in range(2):
            steps = [turned_s[2 * p + half, q * LINES : (q + 1) * LINES, :] for p in range(8)]
            lhs = jnp.concatenate(steps, axis=0).astype(BF16)
            part = jnp.dot(lhs, wo[q, half], preferred_element_type=F32)
            near = part if near is None else near + part
    for p in range(8):
        for y in range(2):
            first = p * LINES + y * STEPS
            out[pl.ds(2 * p + y, STEPS, stride=16), :] = near[first : first + STEPS]


def vmem(count):
    return [pl.BlockSpec(memory_space=pltpu.VMEM)] * count


def prepare(*weights):
    shapes = [
        jax.ShapeDtypeStruct((6, VEC, E), F32),
        jax.ShapeDtypeStruct((N, E, E), F32),
        jax.ShapeDtypeStruct((6, 2 * E, 2 * E), BF16),
        jax.ShapeDtypeStruct((2 * C, 4 * E), BF16),
        jax.ShapeDtypeStruct((2 * E, 2 * C), BF16),
        jax.ShapeDtypeStruct((1, 2 * C), F32),
        jax.ShapeDtypeStruct((256, 256), BF16),
        jax.ShapeDtypeStruct((2, ROWS, EQ, E), F32),
        jax.ShapeDtypeStruct((2 * EQ, Q * C), BF16),
        jax.ShapeDtypeStruct((2, SEL, E), BF16),
        jax.ShapeDtypeStruct((Q, 2, EQ, 2 * C), BF16),
    ]
    ready = pl.pallas_call(
        prepare_kernel,
        out_shape=shapes,
        in_specs=[pl.BlockSpec(memory_space=pltpu.VMEM if i == XW else pl.ANY) for i in range(10)],
        out_specs=vmem(11),
        scratch_shapes=[pltpu.VMEM(w.shape, w.dtype) for i, w in enumerate(weights) if i != XW] + [pltpu.SemaphoreType.DMA((9,))],
        compiler_params=PARAMS,
        name="prepare",
    )(*[w if i == XW else pltpu.with_memory_space_constraint(w, pltpu.HBM) for i, w in enumerate(weights)])
    return ready[:7], (*ready[7:], ready[5])


def planes(values, ready):
    return pl.pallas_call(
        plane_kernel,
        out_shape=jax.ShapeDtypeStruct((256, 2 * C), BF16),
        in_specs=vmem(8),
        out_specs=vmem(1)[0],
        scratch_shapes=[
            pltpu.VMEM((2, 704, E), F32),
            pltpu.VMEM((256, E), BF16),
            pltpu.VMEM((16, E, E), F32),
            pltpu.VMEM((16, E, E), BF16),
            pltpu.VMEM((4, E, E), F32),
            pltpu.VMEM((16, E, E), F32),
            pltpu.VMEM((16, E, E), F32),
            pltpu.VMEM((16 * 2 * N, E), F32),
            pltpu.VMEM((16, E, E), BF16),
            pltpu.VMEM((2, 2, 512, E), F32),
        ],
        compiler_params=PARAMS,
        name="planes",
    )(values, *ready)


def z_inputs(values, ready):
    table, lhsq, xp, _, gain2 = ready
    return pl.pallas_call(
        line_inputs_kernel,
        out_shape=[
            jax.ShapeDtypeStruct((STEPS, EQ, E), F32),
            jax.ShapeDtypeStruct((2, STEPS, SEL, E), F32),
            jax.ShapeDtypeStruct((2, STEPS, EQ, E), F32),
            jax.ShapeDtypeStruct((2, STEPS, EQ, E), F32),
            jax.ShapeDtypeStruct((STEPS, EQ, E), F32),
        ],
        in_specs=vmem(5),
        out_specs=vmem(5),
        scratch_shapes=[pltpu.VMEM((256, E), F32), pltpu.VMEM((256, E), F32), pltpu.VMEM((STEPS, EQ, E), F32)],
        compiler_params=PARAMS,
        name="z_inputs",
    )(values, table, lhsq, xp, gain2)


def z_lines(given, ready):
    table, _, _, wo, _ = ready
    return pl.pallas_call(
        line_scan_kernel,
        out_shape=jax.ShapeDtypeStruct((256, 2 * C), F32),
        in_specs=vmem(7),
        out_specs=vmem(1)[0],
        scratch_shapes=[pltpu.VMEM((STEPS, EQ, E), F32), pltpu.VMEM((STEPS, E, EQ), F32)],
        compiler_params=PARAMS,
        name="z_lines",
    )(table, wo, *given)


def local(voxels, norm_gain, in_weight, conv_weight, conv_bias, x_weight, dt_weight, dt_bias, a_rate, skip_gain, out_weight):
    pairs = voxels.reshape(2, 128, 2 * C)
    sent = pairs.transpose(1, 0, 2)
    arrived = lax.all_to_all(sent, ("row", "col"), split_axis=0, concat_axis=0, tiled=True)
    ready, z_ready = prepare(
        in_weight,
        conv_weight,
        conv_bias,
        x_weight.transpose(0, 2, 1),
        dt_weight,
        dt_bias,
        a_rate.transpose(0, 2, 1),
        skip_gain,
        out_weight.T,
        norm_gain.reshape(1, C),
    )
    given = z_inputs(pairs.reshape(256, 2 * C), z_ready)
    far = planes(arrived.reshape(256, 2 * C), ready)
    returned = lax.all_to_all(far.reshape(128, 2, 2 * C), ("row", "col"), split_axis=0, concat_axis=0, tiled=True)
    near = z_lines(given, z_ready)
    mixed = (near.reshape(128, 2, 2 * C) + returned.astype(F32)).astype(BF16)
    return mixed.transpose(1, 0, 2).reshape(1, 2, 128 * 2 * C)


def solution(mesh):
    in_specs = (P("row", "col", None),) + (P(),) * 10
    return jax.shard_map(local, mesh=mesh, in_specs=in_specs, out_specs=P("row", "col", None), check_vma=False)
```

```python
import math

import jax
import jax.numpy as jnp
from jax import lax
from jax.experimental import pallas as pl
from jax.experimental.pallas import tpu as pltpu
from jax.sharding import PartitionSpec as P

C = 64
E = 128
N = 16
R = 4
K = 4
PAD = 8
CW, CB, DB, SK, VEC = 0, 4, 5, 6, 8
Q = 4
EQ = E // Q
STEPS = 16
LINES = 32
A0, CW0, DW0, CB0, DB0, SK0, ROWS = 0, 16, 20, 24, 25, 26, 32
XW = 3
SEL = 48
LN2 = math.log(2.0)
LOG2E = 1.0 / LN2
F32 = jnp.float32
BF16 = jnp.bfloat16
HIGHEST = lax.Precision.HIGHEST
NT = (((1,), (1,)), ((), ()))
TN = (((0,), (0,)), ((), ()))
PARAMS = pltpu.CompilerParams(vmem_limit_bytes=48 * 1024 * 1024)


def iota(shape, axis):
    return lax.broadcasted_iota(jnp.int32, shape, axis)


def silu(x):
    half = 0.5 * x
    return half * (1.0 + jnp.tanh(half))


def softplus2(x):
    tail = jnp.exp2(-jnp.abs(x))
    return jnp.maximum(x, 0.0) + jnp.where(tail < 1e-4, tail * LOG2E, jnp.log2(1.0 + tail))


def prepare_kernel(*refs):
    given, (vec, rate_far, w_step, w_in, w_out, gain2, swap), (table, lhsq, xp, wo) = refs[:10], refs[10:17], refs[17:21]
    here, sem = refs[21:30], refs[30]
    names = [i for i in range(10) if i != XW]
    copies = [pltpu.make_async_copy(given[i], here[at], sem.at[at]) for at, i in enumerate(names)]
    for copy in copies:
        copy.start()
    for copy in copies:
        copy.wait()
    in_w, conv_w, conv_b, dt_w, dt_b, rate, skip, out_w, gain = here
    x_w = given[XW]
    row, column = iota((R + 2 * N, E), 0), iota((R + 2 * N, E), 1)
    pick = (row == column % (2 * N) + R).astype(F32)
    for d in range(2, 6):
        vec[d, CW : CW + K] = conv_w[d] * 0.5
        vec[d, CB : CB + 1] = conv_b[d : d + 1, :] * 0.5
        vec[d, DB : DB + 1] = dt_b[d : d + 1, :] * LOG2E
        vec[d, SK : SK + 1] = skip[d : d + 1, :]
        vec[d, SK + 1 :] = jnp.zeros((1, E), F32)
        given_w = x_w[d].astype(F32)
        both = lax.dot_general(given_w[:R], dt_w[d] * LOG2E, TN, precision=HIGHEST, preferred_element_type=F32)
        high = both.astype(BF16)
        w_step[d, 0:E, 0:E] = high
        w_step[d, E:, 0:E] = (both - high.astype(F32)).astype(BF16)
        w_step[d, 0:E, E:] = lax.dot_general(given_w, pick, TN, preferred_element_type=F32).astype(BF16)
        w_step[d, E:, E:] = jnp.zeros((E, E), BF16)
    row, column = iota((256, 256), 0), iota((256, 256), 1)
    swap[...] = (column == row % 16 * 16 + row // 16).astype(BF16)
    turned = jnp.concatenate([-rate[2 + i] for i in range(4)], axis=0).T
    high = turned.astype(BF16)
    both = jnp.concatenate([high, (turned - high.astype(F32)).astype(BF16)], axis=1)
    row, column = iota((8 * N, E), 0), iota((8 * N, E), 1)
    for n in range(N):
        chosen = ((row % N == n) & (row // N % 4 == column // 32)).astype(BF16)
        rate_far[n] = jnp.dot(both, chosen, preferred_element_type=F32)
    weight = in_w[...]
    zero = jnp.zeros((C, E), BF16)
    inner, gate = weight[:, :E], weight[:, E:]
    w_in[0:C] = jnp.concatenate([inner, zero, gate, zero], axis=1)
    w_in[C:] = jnp.concatenate([zero, inner, zero, gate], axis=1)
    turned = out_w[...].astype(F32)
    wide = jnp.concatenate([turned, turned], axis=0).T
    low_half = iota((E, 2 * C), 1) < C
    w_out[0:E] = jnp.where(low_half, wide, 0.0).astype(BF16)
    w_out[E:] = jnp.where(low_half, 0.0, wide).astype(BF16)
    gain2[...] = jnp.concatenate([gain[...], gain[...]], axis=1)
    mask = ((iota((EQ, E), 1) % EQ) == iota((EQ, E), 0)).astype(BF16)
    same = (iota((2 * E, E), 0) % E // EQ == iota((2 * E, E), 1) // EQ).astype(BF16)
    row, column = iota((SEL, 36), 0), iota((SEL, 36), 1)
    pick = (column == jnp.where(row < 2 * N, row + R, row - 2 * N)) & (row < 2 * N + R)
    pick = pick.astype(BF16)
    for d in range(2):
        rows = jnp.concatenate(
            [
                rate[d] * (-LOG2E),
                conv_w[d],
                dt_w[d],
                conv_b[d : d + 1, :],
                dt_b[d : d + 1, :],
                skip[d : d + 1, :],
                jnp.zeros((5, E), F32),
            ],
            axis=0,
        )
        high = rows.astype(BF16)
        rest = (rows - high.astype(F32)).astype(BF16)
        spread = jnp.concatenate(
            [(part[:, None, :] * mask[None]).reshape(ROWS * EQ, E) for part in (high, rest)], axis=1
        )
        table[d] = jnp.dot(spread, same, preferred_element_type=F32).reshape(ROWS, EQ, E)
        xp[d] = jnp.dot(pick, x_w[d], preferred_element_type=F32).astype(BF16)
    turned = in_w[...].astype(F32).T
    for part in range(2):
        blocks = [turned[part * E + q * EQ : part * E + (q + 1) * EQ] for q in range(Q)]
        lhsq[part * EQ : (part + 1) * EQ, :] = jnp.concatenate(blocks, axis=1).astype(BF16)
    for q in range(Q):
        for half in range(2):
            wo[q, half] = w_out[half * E + q * EQ : half * E + (q + 1) * EQ, :]


def enter(values, gain2):
    squares = values * values
    high = squares.astype(BF16)
    rest = (squares - high.astype(F32)).astype(BF16)
    block = iota((4 * C, 2 * C), 0) % (2 * C) // C == iota((4 * C, 2 * C), 1) // C
    total = jnp.dot(jnp.concatenate([high, rest], axis=1), block.astype(BF16), preferred_element_type=F32)
    return (values * lax.rsqrt(total * (1.0 / C) + 1e-05) * gain2).astype(BF16)


def leave(first, second, w_out):
    hidden = jnp.concatenate([first.astype(BF16), second.astype(BF16)], axis=1)
    return jnp.dot(hidden, w_out, preferred_element_type=F32)


def step_inputs(taps, vec, w_step):
    half = vec[CB : CB + 1, :]
    for k in range(K):
        half = half + vec[CW + k : CW + k + 1, :] * taps[k]
    act = (half + half * jnp.tanh(half)).astype(BF16)
    both = jnp.dot(jnp.concatenate([act, act], axis=1), w_step, preferred_element_type=F32)
    return act, softplus2(both[:, :E] + vec[DB : DB + 1, :]), both[:, E:]


def tree_sum(terms):
    while len(terms) > 1:
        terms = [terms[i] + terms[i + 1] for i in range(0, len(terms), 2)]
    return terms[0]


def plane_kernel(values, vec, rate_far, w_step, w_in, w_out, gain2, swap, out, lines_s, normed_s, step_s, act_s, sel_s, step_t, fresh_t, sel_t, y_s, direct_s):
    normed = enter(values[...].astype(F32), gain2[...])
    normed_s[...] = normed
    both = jnp.dot(normed, w_in[:, : 2 * E], preferred_element_type=F32).astype(BF16)
    inner = [both[:, h * E : (h + 1) * E].astype(F32) for h in range(2)]
    swapped = jnp.dot(swap[...], both, preferred_element_type=F32)
    zero = jnp.zeros((96, E), F32)
    for axis in range(2):
        lines_s[axis, 0:96, :] = zero
        lines_s[axis, 608:704, :] = zero
    for h in range(2):
        for i in range(16):
            first = 96 + i * 32 + h * 16
            lines_s[1, first : first + 16, :] = inner[h][i * 16 : (i + 1) * 16]
            lines_s[0, first : first + 16, :] = swapped[i * 16 : (i + 1) * 16, h * E : (h + 1) * E]

    eye = (iota((E, E), 0) == iota((E, E), 1)).astype(BF16)
    for part in range(4):
        for axis in range(2):
            for d in range(2):
                index = 2 + 2 * axis + d
                begin = 4 * part if d == 0 else 12 - 4 * part
                firsts = [32 * (begin + (k if d == 0 else 6 - k)) for k in range(K)]
                taps = [lines_s[axis, first : first + 128, :] for first in firsts]
                act, step, sel = step_inputs(taps, vec[index], w_step[index])
                direct_s[axis, d, begin * 32 : begin * 32 + 128, :] = vec[index, SK : SK + 1, :] * act.astype(F32)
                rows = slice(axis * 64 + d * 32, axis * 64 + d * 32 + 32)
                for i in range(4):
                    t = i if d == 0 else 3 - i
                    lanes = slice(i * 32, i * 32 + 32)
                    step_s[4 * part + i, rows, :] = step[t * 32 : (t + 1) * 32]
                    act_s[4 * part + i, rows, :] = act[t * 32 : (t + 1) * 32]
                    sel_s[part, rows, lanes] = sel[t * 32 : (t + 1) * 32, lanes]
        for s in range(4 * part, 4 * part + 4):
            step = step_s[s].T
            step_t[s] = step
            fresh_t[s] = step * lax.dot_general(eye, act_s[s], NT, preferred_element_type=F32)
        sel_t[part * 128 : part * 128 + 128, :] = sel_s[part].T

    def group(g, carry):
        first = g * 16 if isinstance(g, int) else pl.multiple_of(g * 16, 16)
        rows = [pl.ds(first + 8 * i, 8) for i in range(2)]
        results = []
        for i in range(2):
            rates = [rate_far[n, rows[i], :] for n in range(N)]
            state = None
            result = []
            for s in range(16):
                step = step_t[s, rows[i], :]
                fresh = fresh_t[s, rows[i], :]
                following = []
                total = [None, None]
                for n in range(N):
                    at = s * 32 + n
                    new = fresh * sel_t[at : at + 1, :]
                    if state is not None:
                        new = new + jnp.exp2(step * rates[n]) * state[n]
                    following.append(new)
                    term = new * sel_t[at + N : at + N + 1, :]
                    total[n % 2] = term if total[n % 2] is None else total[n % 2] + term
                state = following
                result.append(total[0] + total[1])
            results.append(result)
        here = pl.ds(first, 16)
        for s in range(16):
            y_s[s, here, :] = jnp.concatenate([results[0][s], results[1][s]], axis=0).astype(BF16)
        return carry

    group(0, 0)
    lax.fori_loop(1, 7, group, 0)
    group(7, 0)
    gates = silu(jnp.dot(normed_s[...], w_in[:, 2 * E :], preferred_element_type=F32))
    turned = [y_s[s].T.astype(F32) for s in range(16)]
    sums = []
    for axis in range(2):
        rows = []
        for t in range(16):
            both = turned[t][axis * 64 : axis * 64 + 32] + turned[15 - t][axis * 64 + 32 : axis * 64 + 64]
            here = pl.ds(t * 32, 32)
            rows.append(direct_s[axis, 0, here, :] + direct_s[axis, 1, here, :] + both * LN2)
        sums.append(rows)
    halves = [jnp.concatenate([row[h * 16 : (h + 1) * 16] for row in sums[0]], axis=0).astype(BF16) for h in range(2)]
    along_y = jnp.dot(swap[...], jnp.concatenate(halves, axis=1), preferred_element_type=F32)
    hidden = []
    for h in range(2):
        along_x = jnp.concatenate([row[h * 16 : (h + 1) * 16] for row in sums[1]], axis=0)
        hidden.append((along_y[:, h * E : (h + 1) * E] + along_x) * gates[:, h * E : (h + 1) * E])
    out[...] = leave(hidden[0], hidden[1], w_out[...]).astype(BF16)


def z_softplus(x):
    tail = jnp.exp2(jnp.abs(x) * (-LOG2E))
    return jnp.maximum(x, 0.0) + jnp.where(tail < 1e-4, tail, jnp.log(1.0 + tail))


def normalise(values, gain2, plain, rolled):
    low = iota(values.shape, 1) < C
    squares = values * values
    first = jnp.sum(jnp.where(low, squares, 0.0), axis=1, keepdims=True) * (1.0 / C)
    second = jnp.sum(jnp.where(low, 0.0, squares), axis=1, keepdims=True) * (1.0 / C)
    scale = jnp.where(low, lax.rsqrt(first + 1e-05), lax.rsqrt(second + 1e-05))
    normed = (values * scale * gain2).astype(BF16).astype(F32)
    plain[...] = normed
    rolled[...] = pltpu.roll(normed, C, 1)


def project(blocks, lhsq):
    half = jnp.concatenate(blocks, axis=0)
    zero = jnp.zeros_like(half)
    rows = jnp.concatenate(
        [jnp.concatenate([half, zero], axis=1), jnp.concatenate([zero, half], axis=1)], axis=0
    ).astype(BF16)
    both = lax.dot_general(lhsq, rows, NT, preferred_element_type=F32)
    return both[:EQ].astype(BF16).astype(F32), both[EQ:]


def z_step(d, index, neighbours, table, xp, quarter, act_s, sel_s, step_s, fresh_s):
    pre = table[index, CB0]
    for k in range(K):
        if neighbours[k] is not None:
            pre = pre + table[index, CW0 + k] * neighbours[k]
    act = silu(pre).astype(BF16).astype(F32)
    spread = jnp.concatenate([jnp.where(quarter == q, act, 0.0) for q in range(Q)], axis=0).astype(BF16)
    sel = jnp.dot(xp[index], spread, preferred_element_type=F32)
    sel = sel + pltpu.roll(sel, 64, 1)
    sel = sel + pltpu.roll(sel, 32, 1)
    raw = table[index, DB0]
    for r in range(R):
        raw = raw + table[index, DW0 + r] * sel[2 * N + r : 2 * N + r + 1, :]
    step = z_softplus(raw)
    return act, sel, step


def scan_group(index, d, rows, start, table, sel_s, step_s, fresh_s, y_s):
    rates = [table[index, A0 + n, rows, :] for n in range(N)]
    state = start
    for s in range(STEPS):
        t = s if d == 0 else STEPS - 1 - s
        step = step_s[d, t, rows, :]
        fresh = fresh_s[d, t, rows, :]
        total = [None, None]
        following = []
        for n in range(N):
            new = fresh * sel_s[d, t, n : n + 1, :]
            if state is not None:
                new = new + jnp.exp2(step * rates[n]) * state[n]
            following.append(new)
            term = new * sel_s[d, t, N + n : N + n + 1, :]
            total[n % 2] = term if total[n % 2] is None else total[n % 2] + term
        state = following
        y_s[t, rows, :] = y_s[t, rows, :] + (total[0] + total[1])
    return state


def gated_rows(y_s, gate_s, turned_s):
    for t in range(STEPS):
        turned_s[t] = (y_s[t] * gate_s[t]).T


def line_inputs_kernel(values, table, lhsq_ref, xp, gain2, gate_s, sel_s, step_s, fresh_s, y_s, plain, rolled, inner_s):
    normalise(values[...].astype(F32), gain2[...], plain, rolled)
    lane = iota((EQ, E), 1)
    quarter = lane // LINES
    chunk = lane % STEPS
    low = iota((STEPS, 2 * C), 1) < C
    lhsq = lhsq_ref[...]
    for t in range(STEPS):
        blocks = []
        for half in range(2):
            for y in range(2):
                where = pl.ds(y * 128 + t // 2, STEPS, stride=8)
                rows = plain[where, :] if t % 2 == half else rolled[where, :]
                blocks.append(jnp.where(low, rows, 0.0) if half == 0 else jnp.where(low, 0.0, rows))
        inner, gate = project(blocks, lhsq)
        inner_s[t] = inner
        gate_s[t] = silu(gate)
    for d in range(2):
        edge = (chunk >= 1) if d == 0 else (chunk < STEPS - 1)
        for t in range(STEPS):
            near = []
            for k in range(K):
                p = t - 3 + k if d == 0 else t + 3 - k
                if 0 <= p < STEPS:
                    near.append(inner_s[p])
                else:
                    moved = pltpu.roll(inner_s[p % STEPS], 1 if d == 0 else E - 1, 1)
                    near.append(jnp.where(edge, moved, 0.0))
            act, sel, step = z_step(d, d, near, table, xp, quarter, None, sel_s, step_s, fresh_s)
            sel_s[d, t] = sel
            step_s[d, t] = step
            fresh_s[d, t] = step * act
            direct = table[d, SK0] * act
            y_s[t] = direct if d == 0 else y_s[t] + direct


def line_scan_kernel(table, wo, gate_s, sel_s, step_s, fresh_s, direct_s, out, y_s, turned_s):
    far_off = 1e4
    y_s[...] = direct_s[...]

    def group(g, carry):
        rows = pl.ds(pl.multiple_of(g * 8, 8), 8)
        place = iota((8, E), 1) % STEPS
        for d in range(2):
            rates = [table[d, A0 + n, rows, :] for n in range(N)]
            ends = None
            whole = None
            for s in range(STEPS):
                t = s if d == 0 else STEPS - 1 - s
                step = step_s[d, t, rows, :]
                fresh = fresh_s[d, t, rows, :]
                whole = step if whole is None else whole + step
                following = []
                for n in range(N):
                    new = fresh * sel_s[d, t, n : n + 1, :]
                    if ends is not None:
                        new = new + jnp.exp2(step * rates[n]) * ends[n]
                    following.append(new)
                ends = following
            before = place if d == 0 else STEPS - 1 - place

            def moved(x, k, d=d):
                return pltpu.roll(x, k if d == 0 else E - k, 1)

            def kept(k, x, before=before):
                return jnp.where(before >= k, x, far_off)

            one = moved(whole, 1)
            two = one + moved(whole, 2)
            three = two + moved(whole, 3)
            four = three + moved(whole, 4)
            eight = four + moved(four, 4)
            twelve = eight + moved(four, 8)
            spans = [kept(2, one), kept(3, two), kept(4, three)]
            wide = [kept(4, four), kept(8, eight), kept(12, twelve)]
            start = []
            for n in range(N):
                sums = jnp.where(before >= 1, moved(ends[n], 1), 0.0)
                for k in range(3):
                    sums = sums + jnp.exp2(spans[k] * rates[n]) * moved(ends[n], k + 2)
                start.append(sums)
            for n in range(N):
                sums = start[n]
                for k in range(3):
                    sums = sums + jnp.exp2(wide[k] * rates[n]) * moved(start[n], 4 * k + 4)
                start[n] = sums
            scan_group(d, d, rows, start, table, sel_s, step_s, fresh_s, y_s)
        return carry

    lax.fori_loop(0, EQ // 8, group, 0)
    gated_rows(y_s, gate_s, turned_s)
    near = None
    for q in range(Q):
        for half in range(2):
            steps = [turned_s[2 * p + half, q * LINES : (q + 1) * LINES, :] for p in range(8)]
            lhs = jnp.concatenate(steps, axis=0).astype(BF16)
            part = jnp.dot(lhs, wo[q, half], preferred_element_type=F32)
            near = part if near is None else near + part
    for p in range(8):
        for y in range(2):
            first = p * LINES + y * STEPS
            out[pl.ds(2 * p + y, STEPS, stride=16), :] = near[first : first + STEPS]


def vmem(count):
    return [pl.BlockSpec(memory_space=pltpu.VMEM)] * count


def prepare(*weights):
    shapes = [
        jax.ShapeDtypeStruct((6, VEC, E), F32),
        jax.ShapeDtypeStruct((N, E, E), F32),
        jax.ShapeDtypeStruct((6, 2 * E, 2 * E), BF16),
        jax.ShapeDtypeStruct((2 * C, 4 * E), BF16),
        jax.ShapeDtypeStruct((2 * E, 2 * C), BF16),
        jax.ShapeDtypeStruct((1, 2 * C), F32),
        jax.ShapeDtypeStruct((256, 256), BF16),
        jax.ShapeDtypeStruct((2, ROWS, EQ, E), F32),
        jax.ShapeDtypeStruct((2 * EQ, Q * C), BF16),
        jax.ShapeDtypeStruct((2, SEL, E), BF16),
        jax.ShapeDtypeStruct((Q, 2, EQ, 2 * C), BF16),
    ]
    ready = pl.pallas_call(
        prepare_kernel,
        out_shape=shapes,
        in_specs=[pl.BlockSpec(memory_space=pltpu.VMEM if i == XW else pl.ANY) for i in range(10)],
        out_specs=vmem(11),
        scratch_shapes=[pltpu.VMEM(w.shape, w.dtype) for i, w in enumerate(weights) if i != XW] + [pltpu.SemaphoreType.DMA((9,))],
        compiler_params=PARAMS,
        name="prepare",
    )(*[w if i == XW else pltpu.with_memory_space_constraint(w, pltpu.HBM) for i, w in enumerate(weights)])
    return ready[:7], (*ready[7:], ready[5])


def planes(values, ready):
    return pl.pallas_call(
        plane_kernel,
        out_shape=jax.ShapeDtypeStruct((256, 2 * C), BF16),
        in_specs=vmem(8),
        out_specs=vmem(1)[0],
        scratch_shapes=[
            pltpu.VMEM((2, 704, E), F32),
            pltpu.VMEM((256, E), BF16),
            pltpu.VMEM((16, E, E), F32),
            pltpu.VMEM((16, E, E), BF16),
            pltpu.VMEM((4, E, E), F32),
            pltpu.VMEM((16, E, E), F32),
            pltpu.VMEM((16, E, E), F32),
            pltpu.VMEM((16 * 2 * N, E), F32),
            pltpu.VMEM((16, E, E), BF16),
            pltpu.VMEM((2, 2, 512, E), F32),
        ],
        compiler_params=PARAMS,
        name="planes",
    )(values, *ready)


def z_inputs(values, ready):
    table, lhsq, xp, _, gain2 = ready
    return pl.pallas_call(
        line_inputs_kernel,
        out_shape=[
            jax.ShapeDtypeStruct((STEPS, EQ, E), F32),
            jax.ShapeDtypeStruct((2, STEPS, SEL, E), F32),
            jax.ShapeDtypeStruct((2, STEPS, EQ, E), F32),
            jax.ShapeDtypeStruct((2, STEPS, EQ, E), F32),
            jax.ShapeDtypeStruct((STEPS, EQ, E), F32),
        ],
        in_specs=vmem(5),
        out_specs=vmem(5),
        scratch_shapes=[pltpu.VMEM((256, E), F32), pltpu.VMEM((256, E), F32), pltpu.VMEM((STEPS, EQ, E), F32)],
        compiler_params=PARAMS,
        name="z_inputs",
    )(values, table, lhsq, xp, gain2)


def z_lines(given, ready):
    table, _, _, wo, _ = ready
    return pl.pallas_call(
        line_scan_kernel,
        out_shape=jax.ShapeDtypeStruct((256, 2 * C), F32),
        in_specs=vmem(7),
        out_specs=vmem(1)[0],
        scratch_shapes=[pltpu.VMEM((STEPS, EQ, E), F32), pltpu.VMEM((STEPS, E, EQ), F32)],
        compiler_params=PARAMS,
        name="z_lines",
    )(table, wo, *given)


def local(voxels, norm_gain, in_weight, conv_weight, conv_bias, x_weight, dt_weight, dt_bias, a_rate, skip_gain, out_weight):
    pairs = voxels.reshape(2, 128, 2 * C)
    sent = pairs.transpose(1, 0, 2)
    arrived = lax.all_to_all(sent, ("row", "col"), split_axis=0, concat_axis=0, tiled=True)
    ready, z_ready = prepare(
        in_weight,
        conv_weight,
        conv_bias,
        x_weight.transpose(0, 2, 1),
        dt_weight,
        dt_bias,
        a_rate.transpose(0, 2, 1),
        skip_gain,
        out_weight.T,
        norm_gain.reshape(1, C),
    )
    given = z_inputs(pairs.reshape(256, 2 * C), z_ready)
    far = planes(arrived.reshape(256, 2 * C), ready)
    returned = lax.all_to_all(far.reshape(128, 2, 2 * C), ("row", "col"), split_axis=0, concat_axis=0, tiled=True)
    near = z_lines(given, z_ready)
    mixed = (near.reshape(128, 2, 2 * C) + returned.astype(F32)).astype(BF16)
    return mixed.transpose(1, 0, 2).reshape(1, 2, 128 * 2 * C)


def solution(mesh):
    in_specs = (P("row", "col", None),) + (P(),) * 10
    return jax.shard_map(local, mesh=mesh, in_specs=in_specs, out_specs=P("row", "col", None), check_vma=False)
```

```python
import math

import jax
import jax.numpy as jnp
from jax import lax
from jax.experimental import pallas as pl
from jax.experimental.pallas import tpu as pltpu
from jax.sharding import PartitionSpec as P

C = 64
E = 128
N = 16
R = 4
K = 4
PAD = 8
CW, CB, DB, SK, VEC = 0, 4, 5, 6, 8
Q = 4
EQ = E // Q
STEPS = 16
LINES = 32
A0, CW0, DW0, CB0, DB0, SK0, ROWS = 0, 16, 20, 24, 25, 26, 32
XW = 3
SEL = 48
LN2 = math.log(2.0)
LOG2E = 1.0 / LN2
F32 = jnp.float32
BF16 = jnp.bfloat16
HIGHEST = lax.Precision.HIGHEST
NT = (((1,), (1,)), ((), ()))
TN = (((0,), (0,)), ((), ()))
PARAMS = pltpu.CompilerParams(vmem_limit_bytes=48 * 1024 * 1024)


def iota(shape, axis):
    return lax.broadcasted_iota(jnp.int32, shape, axis)


def silu(x):
    half = 0.5 * x
    return half * (1.0 + jnp.tanh(half))


def softplus2(x):
    tail = jnp.exp2(-jnp.abs(x))
    return jnp.maximum(x, 0.0) + jnp.where(tail < 1e-4, tail * LOG2E, jnp.log2(1.0 + tail))


def prepare_kernel(*refs):
    given, (vec, rate_far, w_step, w_in, w_out, gain2, swap), (table, lhsq, xp, wo) = refs[:10], refs[10:17], refs[17:21]
    here, sem = refs[21:30], refs[30]
    names = [i for i in range(10) if i != XW]
    copies = [pltpu.make_async_copy(given[i], here[at], sem.at[at]) for at, i in enumerate(names)]
    for copy in copies:
        copy.start()
    for copy in copies:
        copy.wait()
    in_w, conv_w, conv_b, dt_w, dt_b, rate, skip, out_w, gain = here
    x_w = given[XW]
    row, column = iota((R + 2 * N, E), 0), iota((R + 2 * N, E), 1)
    pick = (row == column % (2 * N) + R).astype(F32)
    for d in range(2, 6):
        vec[d, CW : CW + K] = conv_w[d] * 0.5
        vec[d, CB : CB + 1] = conv_b[d : d + 1, :] * 0.5
        vec[d, DB : DB + 1] = dt_b[d : d + 1, :] * LOG2E
        vec[d, SK : SK + 1] = skip[d : d + 1, :]
        vec[d, SK + 1 :] = jnp.zeros((1, E), F32)
        given_w = x_w[d].astype(F32)
        both = lax.dot_general(given_w[:R], dt_w[d] * LOG2E, TN, precision=HIGHEST, preferred_element_type=F32)
        high = both.astype(BF16)
        w_step[d, 0:E, 0:E] = high
        w_step[d, E:, 0:E] = (both - high.astype(F32)).astype(BF16)
        w_step[d, 0:E, E:] = lax.dot_general(given_w, pick, TN, preferred_element_type=F32).astype(BF16)
        w_step[d, E:, E:] = jnp.zeros((E, E), BF16)
    row, column = iota((256, 256), 0), iota((256, 256), 1)
    swap[...] = (column == row % 16 * 16 + row // 16).astype(BF16)
    turned = jnp.concatenate([-rate[2 + i] for i in range(4)], axis=0).T
    high = turned.astype(BF16)
    both = jnp.concatenate([high, (turned - high.astype(F32)).astype(BF16)], axis=1)
    row, column = iota((8 * N, E), 0), iota((8 * N, E), 1)
    for n in range(N):
        chosen = ((row % N == n) & (row // N % 4 == column // 32)).astype(BF16)
        rate_far[n] = jnp.dot(both, chosen, preferred_element_type=F32)
    weight = in_w[...]
    zero = jnp.zeros((C, E), BF16)
    inner, gate = weight[:, :E], weight[:, E:]
    w_in[0:C] = jnp.concatenate([inner, zero, gate, zero], axis=1)
    w_in[C:] = jnp.concatenate([zero, inner, zero, gate], axis=1)
    turned = out_w[...].astype(F32)
    wide = jnp.concatenate([turned, turned], axis=0).T
    low_half = iota((E, 2 * C), 1) < C
    w_out[0:E] = jnp.where(low_half, wide, 0.0).astype(BF16)
    w_out[E:] = jnp.where(low_half, 0.0, wide).astype(BF16)
    gain2[...] = jnp.concatenate([gain[...], gain[...]], axis=1)
    mask = ((iota((EQ, E), 1) % EQ) == iota((EQ, E), 0)).astype(BF16)
    same = (iota((2 * E, E), 0) % E // EQ == iota((2 * E, E), 1) // EQ).astype(BF16)
    row, column = iota((SEL, 36), 0), iota((SEL, 36), 1)
    pick = (column == jnp.where(row < 2 * N, row + R, row - 2 * N)) & (row < 2 * N + R)
    pick = pick.astype(BF16)
    for d in range(2):
        rows = jnp.concatenate(
            [
                rate[d] * (-LOG2E),
                conv_w[d],
                dt_w[d],
                conv_b[d : d + 1, :],
                dt_b[d : d + 1, :],
                skip[d : d + 1, :],
                jnp.zeros((5, E), F32),
            ],
            axis=0,
        )
        high = rows.astype(BF16)
        rest = (rows - high.astype(F32)).astype(BF16)
        spread = jnp.concatenate(
            [(part[:, None, :] * mask[None]).reshape(ROWS * EQ, E) for part in (high, rest)], axis=1
        )
        table[d] = jnp.dot(spread, same, preferred_element_type=F32).reshape(ROWS, EQ, E)
        xp[d] = jnp.dot(pick, x_w[d], preferred_element_type=F32).astype(BF16)
    turned = in_w[...].astype(F32).T
    for part in range(2):
        blocks = [turned[part * E + q * EQ : part * E + (q + 1) * EQ] for q in range(Q)]
        lhsq[part * EQ : (part + 1) * EQ, :] = jnp.concatenate(blocks, axis=1).astype(BF16)
    for q in range(Q):
        for half in range(2):
            wo[q, half] = w_out[half * E + q * EQ : half * E + (q + 1) * EQ, :]


def enter(values, gain2):
    squares = values * values
    high = squares.astype(BF16)
    rest = (squares - high.astype(F32)).astype(BF16)
    block = iota((4 * C, 2 * C), 0) % (2 * C) // C == iota((4 * C, 2 * C), 1) // C
    total = jnp.dot(jnp.concatenate([high, rest], axis=1), block.astype(BF16), preferred_element_type=F32)
    return (values * lax.rsqrt(total * (1.0 / C) + 1e-05) * gain2).astype(BF16)


def leave(first, second, w_out):
    hidden = jnp.concatenate([first.astype(BF16), second.astype(BF16)], axis=1)
    return jnp.dot(hidden, w_out, preferred_element_type=F32)


def step_inputs(taps, vec, w_step):
    half = vec[CB : CB + 1, :]
    for k in range(K):
        half = half + vec[CW + k : CW + k + 1, :] * taps[k]
    act = (half + half * jnp.tanh(half)).astype(BF16)
    both = jnp.dot(jnp.concatenate([act, act], axis=1), w_step, preferred_element_type=F32)
    return act, softplus2(both[:, :E] + vec[DB : DB + 1, :]), both[:, E:]


def tree_sum(terms):
    while len(terms) > 1:
        terms = [terms[i] + terms[i + 1] for i in range(0, len(terms), 2)]
    return terms[0]


def plane_kernel(values, vec, rate_far, w_step, w_in, w_out, gain2, swap, out, lines_s, normed_s, step_s, act_s, sel_s, step_t, fresh_t, sel_t, y_s, direct_s):
    normed = enter(values[...].astype(F32), gain2[...])
    normed_s[...] = normed
    both = jnp.dot(normed, w_in[:, : 2 * E], preferred_element_type=F32).astype(BF16)
    inner = [both[:, h * E : (h + 1) * E].astype(F32) for h in range(2)]
    swapped = jnp.dot(swap[...], both, preferred_element_type=F32)
    zero = jnp.zeros((96, E), F32)
    for axis in range(2):
        lines_s[axis, 0:96, :] = zero
        lines_s[axis, 608:704, :] = zero
    for h in range(2):
        for i in range(16):
            first = 96 + i * 32 + h * 16
            lines_s[1, first : first + 16, :] = inner[h][i * 16 : (i + 1) * 16]
            lines_s[0, first : first + 16, :] = swapped[i * 16 : (i + 1) * 16, h * E : (h + 1) * E]

    for part in range(4):
        for axis in range(2):
            for d in range(2):
                index = 2 + 2 * axis + d
                begin = 4 * part if d == 0 else 12 - 4 * part
                firsts = [32 * (begin + (k if d == 0 else 6 - k)) for k in range(K)]
                taps = [lines_s[axis, first : first + 128, :] for first in firsts]
                act, step, sel = step_inputs(taps, vec[index], w_step[index])
                direct_s[axis, d, begin * 32 : begin * 32 + 128, :] = vec[index, SK : SK + 1, :] * act.astype(F32)
                rows = slice(axis * 64 + d * 32, axis * 64 + d * 32 + 32)
                for i in range(4):
                    t = i if d == 0 else 3 - i
                    lanes = slice(i * 32, i * 32 + 32)
                    step_s[4 * part + i, rows, :] = step[t * 32 : (t + 1) * 32]
                    act_s[4 * part + i, rows, :] = act[t * 32 : (t + 1) * 32]
                    sel_s[part, rows, lanes] = sel[t * 32 : (t + 1) * 32, lanes]
        for s in range(4 * part, 4 * part + 4):
            step = step_s[s].T
            step_t[s] = step
            fresh_t[s] = step * act_s[s].T.astype(F32)
        sel_t[part * 128 : part * 128 + 128, :] = sel_s[part].T

    def group(g, carry):
        rows = [pl.ds(pl.multiple_of(g * 16 + 8 * i, 8), 8) for i in range(2)]
        results = []
        for i in range(2):
            rates = [rate_far[n, rows[i], :] for n in range(N)]
            state = None
            result = []
            for s in range(16):
                step = step_t[s, rows[i], :]
                fresh = fresh_t[s, rows[i], :]
                following = []
                total = [None, None]
                for n in range(N):
                    at = s * 32 + n
                    new = fresh * sel_t[at : at + 1, :]
                    if state is not None:
                        new = new + jnp.exp2(step * rates[n]) * state[n]
                    following.append(new)
                    term = new * sel_t[at + N : at + N + 1, :]
                    total[n % 2] = term if total[n % 2] is None else total[n % 2] + term
                state = following
                result.append(total[0] + total[1])
            results.append(result)
        here = pl.ds(pl.multiple_of(g * 16, 16), 16)
        for s in range(16):
            y_s[s, here, :] = jnp.concatenate([results[0][s], results[1][s]], axis=0).astype(BF16)
        return carry

    lax.fori_loop(0, 8, group, 0)
    gates = silu(jnp.dot(normed_s[...], w_in[:, 2 * E :], preferred_element_type=F32))
    turned = [y_s[s].T.astype(F32) for s in range(16)]
    sums = []
    for axis in range(2):
        rows = []
        for t in range(16):
            both = turned[t][axis * 64 : axis * 64 + 32] + turned[15 - t][axis * 64 + 32 : axis * 64 + 64]
            here = pl.ds(t * 32, 32)
            rows.append(direct_s[axis, 0, here, :] + direct_s[axis, 1, here, :] + both * LN2)
        sums.append(rows)
    halves = [jnp.concatenate([row[h * 16 : (h + 1) * 16] for row in sums[0]], axis=0).astype(BF16) for h in range(2)]
    along_y = jnp.dot(swap[...], jnp.concatenate(halves, axis=1), preferred_element_type=F32)
    hidden = []
    for h in range(2):
        along_x = jnp.concatenate([row[h * 16 : (h + 1) * 16] for row in sums[1]], axis=0)
        hidden.append((along_y[:, h * E : (h + 1) * E] + along_x) * gates[:, h * E : (h + 1) * E])
    out[...] = leave(hidden[0], hidden[1], w_out[...]).astype(BF16)


def z_softplus(x):
    tail = jnp.exp2(jnp.abs(x) * (-LOG2E))
    return jnp.maximum(x, 0.0) + jnp.where(tail < 1e-4, tail, jnp.log(1.0 + tail))


def normalise(values, gain2, plain, rolled):
    low = iota(values.shape, 1) < C
    squares = values * values
    first = jnp.sum(jnp.where(low, squares, 0.0), axis=1, keepdims=True) * (1.0 / C)
    second = jnp.sum(jnp.where(low, 0.0, squares), axis=1, keepdims=True) * (1.0 / C)
    scale = jnp.where(low, lax.rsqrt(first + 1e-05), lax.rsqrt(second + 1e-05))
    normed = (values * scale * gain2).astype(BF16).astype(F32)
    plain[...] = normed
    rolled[...] = pltpu.roll(normed, C, 1)


def project(blocks, lhsq):
    half = jnp.concatenate(blocks, axis=0)
    zero = jnp.zeros_like(half)
    rows = jnp.concatenate(
        [jnp.concatenate([half, zero], axis=1), jnp.concatenate([zero, half], axis=1)], axis=0
    ).astype(BF16)
    both = lax.dot_general(lhsq, rows, NT, preferred_element_type=F32)
    return both[:EQ].astype(BF16).astype(F32), both[EQ:]


def z_step(d, index, neighbours, table, xp, quarter, act_s, sel_s, step_s, fresh_s):
    pre = table[index, CB0]
    for k in range(K):
        if neighbours[k] is not None:
            pre = pre + table[index, CW0 + k] * neighbours[k]
    act = silu(pre).astype(BF16).astype(F32)
    spread = jnp.concatenate([jnp.where(quarter == q, act, 0.0) for q in range(Q)], axis=0).astype(BF16)
    sel = jnp.dot(xp[index], spread, preferred_element_type=F32)
    sel = sel + pltpu.roll(sel, 64, 1)
    sel = sel + pltpu.roll(sel, 32, 1)
    raw = table[index, DB0]
    for r in range(R):
        raw = raw + table[index, DW0 + r] * sel[2 * N + r : 2 * N + r + 1, :]
    step = z_softplus(raw)
    return act, sel, step


def scan_group(index, d, rows, start, table, sel_s, step_s, fresh_s, y_s):
    rates = [table[index, A0 + n, rows, :] for n in range(N)]
    state = start
    for s in range(STEPS):
        t = s if d == 0 else STEPS - 1 - s
        step = step_s[d, t, rows, :]
        fresh = fresh_s[d, t, rows, :]
        total = [None, None]
        following = []
        for n in range(N):
            new = fresh * sel_s[d, t, n : n + 1, :]
            if state is not None:
                new = new + jnp.exp2(step * rates[n]) * state[n]
            following.append(new)
            term = new * sel_s[d, t, N + n : N + n + 1, :]
            total[n % 2] = term if total[n % 2] is None else total[n % 2] + term
        state = following
        y_s[t, rows, :] = y_s[t, rows, :] + (total[0] + total[1])
    return state


def gated_rows(y_s, gate_s, turned_s):
    for t in range(STEPS):
        turned_s[t] = (y_s[t] * gate_s[t]).T


def line_inputs_kernel(values, table, lhsq_ref, xp, gain2, gate_s, sel_s, step_s, fresh_s, y_s, plain, rolled, inner_s):
    normalise(values[...].astype(F32), gain2[...], plain, rolled)
    lane = iota((EQ, E), 1)
    quarter = lane // LINES
    chunk = lane % STEPS
    low = iota((STEPS, 2 * C), 1) < C
    lhsq = lhsq_ref[...]
    for t in range(STEPS):
        blocks = []
        for half in range(2):
            for y in range(2):
                where = pl.ds(y * 128 + t // 2, STEPS, stride=8)
                rows = plain[where, :] if t % 2 == half else rolled[where, :]
                blocks.append(jnp.where(low, rows, 0.0) if half == 0 else jnp.where(low, 0.0, rows))
        inner, gate = project(blocks, lhsq)
        inner_s[t] = inner
        gate_s[t] = silu(gate)
    for d in range(2):
        edge = (chunk >= 1) if d == 0 else (chunk < STEPS - 1)
        for t in range(STEPS):
            near = []
            for k in range(K):
                p = t - 3 + k if d == 0 else t + 3 - k
                if 0 <= p < STEPS:
                    near.append(inner_s[p])
                else:
                    moved = pltpu.roll(inner_s[p % STEPS], 1 if d == 0 else E - 1, 1)
                    near.append(jnp.where(edge, moved, 0.0))
            act, sel, step = z_step(d, d, near, table, xp, quarter, None, sel_s, step_s, fresh_s)
            sel_s[d, t] = sel
            step_s[d, t] = step
            fresh_s[d, t] = step * act
            direct = table[d, SK0] * act
            y_s[t] = direct if d == 0 else y_s[t] + direct


def line_scan_kernel(table, wo, gate_s, sel_s, step_s, fresh_s, direct_s, out, y_s, turned_s):
    far_off = 1e4
    y_s[...] = direct_s[...]

    def group(g, carry):
        rows = pl.ds(pl.multiple_of(g * 8, 8), 8)
        place = iota((8, E), 1) % STEPS
        for d in range(2):
            rates = [table[d, A0 + n, rows, :] for n in range(N)]
            ends = None
            whole = None
            for s in range(STEPS):
                t = s if d == 0 else STEPS - 1 - s
                step = step_s[d, t, rows, :]
                fresh = fresh_s[d, t, rows, :]
                whole = step if whole is None else whole + step
                following = []
                for n in range(N):
                    new = fresh * sel_s[d, t, n : n + 1, :]
                    if ends is not None:
                        new = new + jnp.exp2(step * rates[n]) * ends[n]
                    following.append(new)
                ends = following
            before = place if d == 0 else STEPS - 1 - place

            def moved(x, k, d=d):
                return pltpu.roll(x, k if d == 0 else E - k, 1)

            def kept(k, x, before=before):
                return jnp.where(before >= k, x, far_off)

            one = moved(whole, 1)
            two = one + moved(whole, 2)
            three = two + moved(whole, 3)
            four = three + moved(whole, 4)
            eight = four + moved(four, 4)
            twelve = eight + moved(four, 8)
            spans = [kept(2, one), kept(3, two), kept(4, three)]
            wide = [kept(4, four), kept(8, eight), kept(12, twelve)]
            start = []
            for n in range(N):
                sums = jnp.where(before >= 1, moved(ends[n], 1), 0.0)
                for k in range(3):
                    sums = sums + jnp.exp2(spans[k] * rates[n]) * moved(ends[n], k + 2)
                start.append(sums)
            for n in range(N):
                sums = start[n]
                for k in range(3):
                    sums = sums + jnp.exp2(wide[k] * rates[n]) * moved(start[n], 4 * k + 4)
                start[n] = sums
            scan_group(d, d, rows, start, table, sel_s, step_s, fresh_s, y_s)
        return carry

    lax.fori_loop(0, EQ // 8, group, 0)
    gated_rows(y_s, gate_s, turned_s)
    near = None
    for q in range(Q):
        for half in range(2):
            steps = [turned_s[2 * p + half, q * LINES : (q + 1) * LINES, :] for p in range(8)]
            lhs = jnp.concatenate(steps, axis=0).astype(BF16)
            part = jnp.dot(lhs, wo[q, half], preferred_element_type=F32)
            near = part if near is None else near + part
    for p in range(8):
        for y in range(2):
            first = p * LINES + y * STEPS
            out[pl.ds(2 * p + y, STEPS, stride=16), :] = near[first : first + STEPS]


def vmem(count):
    return [pl.BlockSpec(memory_space=pltpu.VMEM)] * count


def prepare(*weights):
    shapes = [
        jax.ShapeDtypeStruct((6, VEC, E), F32),
        jax.ShapeDtypeStruct((N, E, E), F32),
        jax.ShapeDtypeStruct((6, 2 * E, 2 * E), BF16),
        jax.ShapeDtypeStruct((2 * C, 4 * E), BF16),
        jax.ShapeDtypeStruct((2 * E, 2 * C), BF16),
        jax.ShapeDtypeStruct((1, 2 * C), F32),
        jax.ShapeDtypeStruct((256, 256), BF16),
        jax.ShapeDtypeStruct((2, ROWS, EQ, E), F32),
        jax.ShapeDtypeStruct((2 * EQ, Q * C), BF16),
        jax.ShapeDtypeStruct((2, SEL, E), BF16),
        jax.ShapeDtypeStruct((Q, 2, EQ, 2 * C), BF16),
    ]
    ready = pl.pallas_call(
        prepare_kernel,
        out_shape=shapes,
        in_specs=[pl.BlockSpec(memory_space=pltpu.VMEM if i == XW else pl.ANY) for i in range(10)],
        out_specs=vmem(11),
        scratch_shapes=[pltpu.VMEM(w.shape, w.dtype) for i, w in enumerate(weights) if i != XW] + [pltpu.SemaphoreType.DMA((9,))],
        compiler_params=PARAMS,
        name="prepare",
    )(*[w if i == XW else pltpu.with_memory_space_constraint(w, pltpu.HBM) for i, w in enumerate(weights)])
    return ready[:7], (*ready[7:], ready[5])


def planes(values, ready):
    return pl.pallas_call(
        plane_kernel,
        out_shape=jax.ShapeDtypeStruct((256, 2 * C), BF16),
        in_specs=vmem(8),
        out_specs=vmem(1)[0],
        scratch_shapes=[
            pltpu.VMEM((2, 704, E), F32),
            pltpu.VMEM((256, E), BF16),
            pltpu.VMEM((16, E, E), F32),
            pltpu.VMEM((16, E, E), BF16),
            pltpu.VMEM((4, E, E), F32),
            pltpu.VMEM((16, E, E), F32),
            pltpu.VMEM((16, E, E), F32),
            pltpu.VMEM((16 * 2 * N, E), F32),
            pltpu.VMEM((16, E, E), BF16),
            pltpu.VMEM((2, 2, 512, E), F32),
        ],
        compiler_params=PARAMS,
        name="planes",
    )(values, *ready)


def z_inputs(values, ready):
    table, lhsq, xp, _, gain2 = ready
    return pl.pallas_call(
        line_inputs_kernel,
        out_shape=[
            jax.ShapeDtypeStruct((STEPS, EQ, E), F32),
            jax.ShapeDtypeStruct((2, STEPS, SEL, E), F32),
            jax.ShapeDtypeStruct((2, STEPS, EQ, E), F32),
            jax.ShapeDtypeStruct((2, STEPS, EQ, E), F32),
            jax.ShapeDtypeStruct((STEPS, EQ, E), F32),
        ],
        in_specs=vmem(5),
        out_specs=vmem(5),
        scratch_shapes=[pltpu.VMEM((256, E), F32), pltpu.VMEM((256, E), F32), pltpu.VMEM((STEPS, EQ, E), F32)],
        compiler_params=PARAMS,
        name="z_inputs",
    )(values, table, lhsq, xp, gain2)


def z_lines(given, ready):
    table, _, _, wo, _ = ready
    return pl.pallas_call(
        line_scan_kernel,
        out_shape=jax.ShapeDtypeStruct((256, 2 * C), F32),
        in_specs=vmem(7),
        out_specs=vmem(1)[0],
        scratch_shapes=[pltpu.VMEM((STEPS, EQ, E), F32), pltpu.VMEM((STEPS, E, EQ), F32)],
        compiler_params=PARAMS,
        name="z_lines",
    )(table, wo, *given)


def local(voxels, norm_gain, in_weight, conv_weight, conv_bias, x_weight, dt_weight, dt_bias, a_rate, skip_gain, out_weight):
    pairs = voxels.reshape(2, 128, 2 * C)
    sent = pairs.transpose(1, 0, 2)
    arrived = lax.all_to_all(sent, ("row", "col"), split_axis=0, concat_axis=0, tiled=True)
    ready, z_ready = prepare(
        in_weight,
        conv_weight,
        conv_bias,
        x_weight.transpose(0, 2, 1),
        dt_weight,
        dt_bias,
        a_rate.transpose(0, 2, 1),
        skip_gain,
        out_weight.T,
        norm_gain.reshape(1, C),
    )
    given = z_inputs(pairs.reshape(256, 2 * C), z_ready)
    far = planes(arrived.reshape(256, 2 * C), ready)
    returned = lax.all_to_all(far.reshape(128, 2, 2 * C), ("row", "col"), split_axis=0, concat_axis=0, tiled=True)
    near = z_lines(given, z_ready)
    mixed = (near + returned.reshape(256, 2 * C).astype(F32)).astype(BF16)
    mixed = lax.optimization_barrier(mixed)
    return mixed.reshape(128, 2, 2 * C).transpose(1, 0, 2).reshape(1, 2, 128 * 2 * C)


def solution(mesh):
    in_specs = (P("row", "col", None),) + (P(),) * 10
    return jax.shard_map(local, mesh=mesh, in_specs=in_specs, out_specs=P("row", "col", None), check_vma=False)
```

```python
import math

import jax
import jax.numpy as jnp
from jax import lax
from jax.experimental import pallas as pl
from jax.experimental.pallas import tpu as pltpu
from jax.sharding import PartitionSpec as P

C = 64
E = 128
N = 16
R = 4
K = 4
PAD = 8
CW, CB, DB, SK, VEC = 0, 4, 5, 6, 8
Q = 4
EQ = E // Q
STEPS = 16
LINES = 32
A0, CW0, DW0, CB0, DB0, SK0, ROWS = 0, 16, 20, 24, 25, 26, 32
XW = 3
SEL = 48
LN2 = math.log(2.0)
LOG2E = 1.0 / LN2
F32 = jnp.float32
BF16 = jnp.bfloat16
HIGHEST = lax.Precision.HIGHEST
NT = (((1,), (1,)), ((), ()))
TN = (((0,), (0,)), ((), ()))
PARAMS = pltpu.CompilerParams(vmem_limit_bytes=48 * 1024 * 1024)


def iota(shape, axis):
    return lax.broadcasted_iota(jnp.int32, shape, axis)


def silu(x):
    half = 0.5 * x
    return half * (1.0 + jnp.tanh(half))


def softplus2(x):
    tail = jnp.exp2(-jnp.abs(x))
    return jnp.maximum(x, 0.0) + jnp.where(tail < 1e-4, tail * LOG2E, jnp.log2(1.0 + tail))


def prepare_kernel(*refs):
    given, (vec, rate_far, w_step, w_in, w_out, gain2, swap), (table, lhsq, xp, wo) = refs[:10], refs[10:17], refs[17:21]
    here, sem = refs[21:30], refs[30]
    names = [i for i in range(10) if i != XW]
    copies = [pltpu.make_async_copy(given[i], here[at], sem.at[at]) for at, i in enumerate(names)]
    for copy in copies:
        copy.start()
    for copy in copies:
        copy.wait()
    in_w, conv_w, conv_b, dt_w, dt_b, rate, skip, out_w, gain = here
    x_w = given[XW]
    row, column = iota((R + 2 * N, E), 0), iota((R + 2 * N, E), 1)
    pick = (row == column % (2 * N) + R).astype(F32)
    for d in range(2, 6):
        vec[d, CW : CW + K] = conv_w[d] * 0.5
        vec[d, CB : CB + 1] = conv_b[d : d + 1, :] * 0.5
        vec[d, DB : DB + 1] = dt_b[d : d + 1, :] * LOG2E
        vec[d, SK : SK + 1] = skip[d : d + 1, :]
        vec[d, SK + 1 :] = jnp.zeros((1, E), F32)
        given_w = x_w[d].astype(F32)
        both = lax.dot_general(given_w[:R], dt_w[d] * LOG2E, TN, precision=HIGHEST, preferred_element_type=F32)
        high = both.astype(BF16)
        w_step[d, 0:E, 0:E] = high
        w_step[d, E:, 0:E] = (both - high.astype(F32)).astype(BF16)
        w_step[d, 0:E, E:] = lax.dot_general(given_w, pick, TN, preferred_element_type=F32).astype(BF16)
        w_step[d, E:, E:] = jnp.zeros((E, E), BF16)
    row, column = iota((256, 256), 0), iota((256, 256), 1)
    swap[...] = (column == row % 16 * 16 + row // 16).astype(BF16)
    turned = jnp.concatenate([-rate[2 + i] for i in range(4)], axis=0).T
    high = turned.astype(BF16)
    both = jnp.concatenate([high, (turned - high.astype(F32)).astype(BF16)], axis=1)
    row, column = iota((8 * N, E), 0), iota((8 * N, E), 1)
    for n in range(N):
        chosen = ((row % N == n) & (row // N % 4 == column // 32)).astype(BF16)
        rate_far[n] = jnp.dot(both, chosen, preferred_element_type=F32)
    weight = in_w[...]
    zero = jnp.zeros((C, E), BF16)
    inner, gate = weight[:, :E], weight[:, E:]
    w_in[0:C] = jnp.concatenate([inner, zero, gate, zero], axis=1)
    w_in[C:] = jnp.concatenate([zero, inner, zero, gate], axis=1)
    turned = out_w[...].astype(F32)
    wide = jnp.concatenate([turned, turned], axis=0).T
    low_half = iota((E, 2 * C), 1) < C
    w_out[0:E] = jnp.where(low_half, wide, 0.0).astype(BF16)
    w_out[E:] = jnp.where(low_half, 0.0, wide).astype(BF16)
    gain2[...] = jnp.concatenate([gain[...], gain[...]], axis=1)
    mask = ((iota((EQ, E), 1) % EQ) == iota((EQ, E), 0)).astype(BF16)
    same = (iota((2 * E, E), 0) % E // EQ == iota((2 * E, E), 1) // EQ).astype(BF16)
    row, column = iota((SEL, 36), 0), iota((SEL, 36), 1)
    pick = (column == jnp.where(row < 2 * N, row + R, row - 2 * N)) & (row < 2 * N + R)
    pick = pick.astype(BF16)
    for d in range(2):
        rows = jnp.concatenate(
            [
                rate[d] * (-LOG2E),
                conv_w[d],
                dt_w[d],
                conv_b[d : d + 1, :],
                dt_b[d : d + 1, :],
                skip[d : d + 1, :],
                jnp.zeros((5, E), F32),
            ],
            axis=0,
        )
        high = rows.astype(BF16)
        rest = (rows - high.astype(F32)).astype(BF16)
        spread = jnp.concatenate(
            [(part[:, None, :] * mask[None]).reshape(ROWS * EQ, E) for part in (high, rest)], axis=1
        )
        table[d] = jnp.dot(spread, same, preferred_element_type=F32).reshape(ROWS, EQ, E)
        xp[d] = jnp.dot(pick, x_w[d], preferred_element_type=F32).astype(BF16)
    turned = in_w[...].astype(F32).T
    for part in range(2):
        blocks = [turned[part * E + q * EQ : part * E + (q + 1) * EQ] for q in range(Q)]
        lhsq[part * EQ : (part + 1) * EQ, :] = jnp.concatenate(blocks, axis=1).astype(BF16)
    for q in range(Q):
        for half in range(2):
            wo[q, half] = w_out[half * E + q * EQ : half * E + (q + 1) * EQ, :]


def enter(values, gain2):
    squares = values * values
    high = squares.astype(BF16)
    rest = (squares - high.astype(F32)).astype(BF16)
    block = iota((4 * C, 2 * C), 0) % (2 * C) // C == iota((4 * C, 2 * C), 1) // C
    total = jnp.dot(jnp.concatenate([high, rest], axis=1), block.astype(BF16), preferred_element_type=F32)
    return (values * lax.rsqrt(total * (1.0 / C) + 1e-05) * gain2).astype(BF16)


def leave(first, second, w_out):
    hidden = jnp.concatenate([first.astype(BF16), second.astype(BF16)], axis=1)
    return jnp.dot(hidden, w_out, preferred_element_type=F32)


def step_inputs(taps, vec, w_step):
    half = vec[CB : CB + 1, :]
    for k in range(K):
        half = half + vec[CW + k : CW + k + 1, :] * taps[k]
    act = (half + half * jnp.tanh(half)).astype(BF16)
    both = jnp.dot(jnp.concatenate([act, act], axis=1), w_step, preferred_element_type=F32)
    return act, softplus2(both[:, :E] + vec[DB : DB + 1, :]), both[:, E:]


def tree_sum(terms):
    while len(terms) > 1:
        terms = [terms[i] + terms[i + 1] for i in range(0, len(terms), 2)]
    return terms[0]


def plane_kernel(values, vec, rate_far, w_step, w_in, w_out, gain2, swap, out, lines_s, normed_s, step_s, act_s, sel_s, step_t, fresh_t, sel_t, y_s, direct_s):
    normed = enter(values[...].astype(F32), gain2[...])
    normed_s[...] = normed
    both = jnp.dot(normed, w_in[:, : 2 * E], preferred_element_type=F32).astype(BF16)
    inner = [both[:, h * E : (h + 1) * E].astype(F32) for h in range(2)]
    swapped = jnp.dot(swap[...], both, preferred_element_type=F32)
    zero = jnp.zeros((96, E), F32)
    for axis in range(2):
        lines_s[axis, 0:96, :] = zero
        lines_s[axis, 608:704, :] = zero
    for h in range(2):
        for i in range(16):
            first = 96 + i * 32 + h * 16
            lines_s[1, first : first + 16, :] = inner[h][i * 16 : (i + 1) * 16]
            lines_s[0, first : first + 16, :] = swapped[i * 16 : (i + 1) * 16, h * E : (h + 1) * E]

    eye = (iota((E, E), 0) == iota((E, E), 1)).astype(BF16)
    for part in range(4):
        for axis in (1, 0):
            for d in range(2):
                index = 2 + 2 * axis + d
                begin = 4 * part if d == 0 else 12 - 4 * part
                firsts = [32 * (begin + (k if d == 0 else 6 - k)) for k in range(K)]
                taps = [lines_s[axis, first : first + 128, :] for first in firsts]
                act, step, sel = step_inputs(taps, vec[index], w_step[index])
                direct_s[axis, d, begin * 32 : begin * 32 + 128, :] = vec[index, SK : SK + 1, :] * act.astype(F32)
                rows = slice(axis * 64 + d * 32, axis * 64 + d * 32 + 32)
                for i in range(4):
                    t = i if d == 0 else 3 - i
                    lanes = slice(i * 32, i * 32 + 32)
                    step_s[4 * part + i, rows, :] = step[t * 32 : (t + 1) * 32]
                    act_s[4 * part + i, rows, :] = act[t * 32 : (t + 1) * 32]
                    sel_s[part, rows, lanes] = sel[t * 32 : (t + 1) * 32, lanes]
        for s in range(4 * part, 4 * part + 4):
            step = step_s[s].T
            step_t[s] = step
            fresh_t[s] = step * lax.dot_general(eye, act_s[s], NT, preferred_element_type=F32)
        sel_t[part * 128 : part * 128 + 128, :] = sel_s[part].T

    def group(g, carry):
        first = g * 16 if isinstance(g, int) else pl.multiple_of(g * 16, 16)
        rows = [pl.ds(first + 8 * i, 8) for i in range(2)]
        results = []
        for i in range(2):
            rates = [rate_far[n, rows[i], :] for n in range(N)]
            state = None
            result = []
            for s in range(16):
                step = step_t[s, rows[i], :]
                fresh = fresh_t[s, rows[i], :]
                following = []
                total = [None, None]
                for n in range(N):
                    at = s * 32 + n
                    new = fresh * sel_t[at : at + 1, :]
                    if state is not None:
                        new = new + jnp.exp2(step * rates[n]) * state[n]
                    following.append(new)
                    term = new * sel_t[at + N : at + N + 1, :]
                    total[n % 2] = term if total[n % 2] is None else total[n % 2] + term
                state = following
                result.append(total[0] + total[1])
            results.append(result)
        here = pl.ds(first, 16)
        for s in range(16):
            y_s[s, here, :] = jnp.concatenate([results[0][s], results[1][s]], axis=0).astype(BF16)
        return carry

    group(0, 0)
    lax.fori_loop(1, 7, group, 0)
    group(7, 0)
    gates = silu(jnp.dot(normed_s[...], w_in[:, 2 * E :], preferred_element_type=F32))
    turned = [y_s[s].T.astype(F32) for s in range(16)]
    sums = []
    for axis in range(2):
        rows = []
        for t in range(16):
            both = turned[t][axis * 64 : axis * 64 + 32] + turned[15 - t][axis * 64 + 32 : axis * 64 + 64]
            here = pl.ds(t * 32, 32)
            rows.append(direct_s[axis, 0, here, :] + direct_s[axis, 1, here, :] + both * LN2)
        sums.append(rows)
    halves = [jnp.concatenate([row[h * 16 : (h + 1) * 16] for row in sums[0]], axis=0).astype(BF16) for h in range(2)]
    along_y = jnp.dot(swap[...], jnp.concatenate(halves, axis=1), preferred_element_type=F32)
    hidden = []
    for h in range(2):
        along_x = jnp.concatenate([row[h * 16 : (h + 1) * 16] for row in sums[1]], axis=0)
        hidden.append((along_y[:, h * E : (h + 1) * E] + along_x) * gates[:, h * E : (h + 1) * E])
    out[...] = leave(hidden[0], hidden[1], w_out[...]).astype(BF16)


def z_softplus(x):
    tail = jnp.exp2(jnp.abs(x) * (-LOG2E))
    return jnp.maximum(x, 0.0) + jnp.where(tail < 1e-4, tail, jnp.log(1.0 + tail))


def normalise(values, gain2, plain, rolled):
    low = iota(values.shape, 1) < C
    squares = values * values
    first = jnp.sum(jnp.where(low, squares, 0.0), axis=1, keepdims=True) * (1.0 / C)
    second = jnp.sum(jnp.where(low, 0.0, squares), axis=1, keepdims=True) * (1.0 / C)
    scale = jnp.where(low, lax.rsqrt(first + 1e-05), lax.rsqrt(second + 1e-05))
    normed = (values * scale * gain2).astype(BF16).astype(F32)
    plain[...] = normed
    rolled[...] = pltpu.roll(normed, C, 1)


def project(blocks, lhsq):
    half = jnp.concatenate(blocks, axis=0)
    zero = jnp.zeros_like(half)
    rows = jnp.concatenate(
        [jnp.concatenate([half, zero], axis=1), jnp.concatenate([zero, half], axis=1)], axis=0
    ).astype(BF16)
    both = lax.dot_general(lhsq, rows, NT, preferred_element_type=F32)
    return both[:EQ].astype(BF16).astype(F32), both[EQ:]


def z_step(d, index, neighbours, table, xp, quarter, act_s, sel_s, step_s, fresh_s):
    pre = table[index, CB0]
    for k in range(K):
        if neighbours[k] is not None:
            pre = pre + table[index, CW0 + k] * neighbours[k]
    act = silu(pre).astype(BF16).astype(F32)
    spread = jnp.concatenate([jnp.where(quarter == q, act, 0.0) for q in range(Q)], axis=0).astype(BF16)
    sel = jnp.dot(xp[index], spread, preferred_element_type=F32)
    sel = sel + pltpu.roll(sel, 64, 1)
    sel = sel + pltpu.roll(sel, 32, 1)
    raw = table[index, DB0]
    for r in range(R):
        raw = raw + table[index, DW0 + r] * sel[2 * N + r : 2 * N + r + 1, :]
    step = z_softplus(raw)
    return act, sel, step


def scan_group(index, d, rows, start, table, sel_s, step_s, fresh_s, y_s):
    rates = [table[index, A0 + n, rows, :] for n in range(N)]
    state = start
    for s in range(STEPS):
        t = s if d == 0 else STEPS - 1 - s
        step = step_s[d, t, rows, :]
        fresh = fresh_s[d, t, rows, :]
        total = [None, None]
        following = []
        for n in range(N):
            new = fresh * sel_s[d, t, n : n + 1, :]
            if state is not None:
                new = new + jnp.exp2(step * rates[n]) * state[n]
            following.append(new)
            term = new * sel_s[d, t, N + n : N + n + 1, :]
            total[n % 2] = term if total[n % 2] is None else total[n % 2] + term
        state = following
        y_s[t, rows, :] = y_s[t, rows, :] + (total[0] + total[1])
    return state


def gated_rows(y_s, gate_s, turned_s):
    for t in range(STEPS):
        turned_s[t] = (y_s[t] * gate_s[t]).T


def line_inputs_kernel(values, table, lhsq_ref, xp, gain2, gate_s, sel_s, step_s, fresh_s, y_s, plain, rolled, inner_s):
    normalise(values[...].astype(F32), gain2[...], plain, rolled)
    lane = iota((EQ, E), 1)
    quarter = lane // LINES
    chunk = lane % STEPS
    low = iota((STEPS, 2 * C), 1) < C
    lhsq = lhsq_ref[...]
    for t in range(STEPS):
        blocks = []
        for half in range(2):
            for y in range(2):
                where = pl.ds(y * 128 + t // 2, STEPS, stride=8)
                rows = plain[where, :] if t % 2 == half else rolled[where, :]
                blocks.append(jnp.where(low, rows, 0.0) if half == 0 else jnp.where(low, 0.0, rows))
        inner, gate = project(blocks, lhsq)
        inner_s[t] = inner
        gate_s[t] = silu(gate)
    for d in range(2):
        edge = (chunk >= 1) if d == 0 else (chunk < STEPS - 1)
        for t in range(STEPS):
            near = []
            for k in range(K):
                p = t - 3 + k if d == 0 else t + 3 - k
                if 0 <= p < STEPS:
                    near.append(inner_s[p])
                else:
                    moved = pltpu.roll(inner_s[p % STEPS], 1 if d == 0 else E - 1, 1)
                    near.append(jnp.where(edge, moved, 0.0))
            act, sel, step = z_step(d, d, near, table, xp, quarter, None, sel_s, step_s, fresh_s)
            sel_s[d, t] = sel
            step_s[d, t] = step
            fresh_s[d, t] = step * act
            direct = table[d, SK0] * act
            y_s[t] = direct if d == 0 else y_s[t] + direct


def line_scan_kernel(table, wo, gate_s, sel_s, step_s, fresh_s, direct_s, out, y_s, turned_s):
    far_off = 1e4
    y_s[...] = direct_s[...]

    def group(g, carry):
        rows = pl.ds(pl.multiple_of(g * 8, 8), 8)
        place = iota((8, E), 1) % STEPS
        for d in range(2):
            rates = [table[d, A0 + n, rows, :] for n in range(N)]
            ends = None
            whole = None
            for s in range(STEPS):
                t = s if d == 0 else STEPS - 1 - s
                step = step_s[d, t, rows, :]
                fresh = fresh_s[d, t, rows, :]
                whole = step if whole is None else whole + step
                following = []
                for n in range(N):
                    new = fresh * sel_s[d, t, n : n + 1, :]
                    if ends is not None:
                        new = new + jnp.exp2(step * rates[n]) * ends[n]
                    following.append(new)
                ends = following
            before = place if d == 0 else STEPS - 1 - place

            def moved(x, k, d=d):
                return pltpu.roll(x, k if d == 0 else E - k, 1)

            def kept(k, x, before=before):
                return jnp.where(before >= k, x, far_off)

            one = moved(whole, 1)
            two = one + moved(whole, 2)
            three = two + moved(whole, 3)
            four = three + moved(whole, 4)
            eight = four + moved(four, 4)
            twelve = eight + moved(four, 8)
            spans = [kept(2, one), kept(3, two), kept(4, three)]
            wide = [kept(4, four), kept(8, eight), kept(12, twelve)]
            start = []
            for n in range(N):
                sums = jnp.where(before >= 1, moved(ends[n], 1), 0.0)
                for k in range(3):
                    sums = sums + jnp.exp2(spans[k] * rates[n]) * moved(ends[n], k + 2)
                start.append(sums)
            for n in range(N):
                sums = start[n]
                for k in range(3):
                    sums = sums + jnp.exp2(wide[k] * rates[n]) * moved(start[n], 4 * k + 4)
                start[n] = sums
            scan_group(d, d, rows, start, table, sel_s, step_s, fresh_s, y_s)
        return carry

    lax.fori_loop(0, EQ // 8, group, 0)
    gated_rows(y_s, gate_s, turned_s)
    near = None
    for q in range(Q):
        for half in range(2):
            steps = [turned_s[2 * p + half, q * LINES : (q + 1) * LINES, :] for p in range(8)]
            lhs = jnp.concatenate(steps, axis=0).astype(BF16)
            part = jnp.dot(lhs, wo[q, half], preferred_element_type=F32)
            near = part if near is None else near + part
    for p in range(8):
        for y in range(2):
            first = p * LINES + y * STEPS
            out[pl.ds(2 * p + y, STEPS, stride=16), :] = near[first : first + STEPS]


def vmem(count):
    return [pl.BlockSpec(memory_space=pltpu.VMEM)] * count


def prepare(*weights):
    shapes = [
        jax.ShapeDtypeStruct((6, VEC, E), F32),
        jax.ShapeDtypeStruct((N, E, E), F32),
        jax.ShapeDtypeStruct((6, 2 * E, 2 * E), BF16),
        jax.ShapeDtypeStruct((2 * C, 4 * E), BF16),
        jax.ShapeDtypeStruct((2 * E, 2 * C), BF16),
        jax.ShapeDtypeStruct((1, 2 * C), F32),
        jax.ShapeDtypeStruct((256, 256), BF16),
        jax.ShapeDtypeStruct((2, ROWS, EQ, E), F32),
        jax.ShapeDtypeStruct((2 * EQ, Q * C), BF16),
        jax.ShapeDtypeStruct((2, SEL, E), BF16),
        jax.ShapeDtypeStruct((Q, 2, EQ, 2 * C), BF16),
    ]
    ready = pl.pallas_call(
        prepare_kernel,
        out_shape=shapes,
        in_specs=[pl.BlockSpec(memory_space=pltpu.VMEM if i == XW else pl.ANY) for i in range(10)],
        out_specs=vmem(11),
        scratch_shapes=[pltpu.VMEM(w.shape, w.dtype) for i, w in enumerate(weights) if i != XW] + [pltpu.SemaphoreType.DMA((9,))],
        compiler_params=PARAMS,
        name="prepare",
    )(*[w if i == XW else pltpu.with_memory_space_constraint(w, pltpu.HBM) for i, w in enumerate(weights)])
    return ready[:7], (*ready[7:], ready[5])


def planes(values, ready):
    return pl.pallas_call(
        plane_kernel,
        out_shape=jax.ShapeDtypeStruct((256, 2 * C), BF16),
        in_specs=vmem(8),
        out_specs=vmem(1)[0],
        scratch_shapes=[
            pltpu.VMEM((2, 704, E), F32),
            pltpu.VMEM((256, E), BF16),
            pltpu.VMEM((16, E, E), F32),
            pltpu.VMEM((16, E, E), BF16),
            pltpu.VMEM((4, E, E), F32),
            pltpu.VMEM((16, E, E), F32),
            pltpu.VMEM((16, E, E), F32),
            pltpu.VMEM((16 * 2 * N, E), F32),
            pltpu.VMEM((16, E, E), BF16),
            pltpu.VMEM((2, 2, 512, E), F32),
        ],
        compiler_params=PARAMS,
        name="planes",
    )(values, *ready)


def z_inputs(values, ready):
    table, lhsq, xp, _, gain2 = ready
    return pl.pallas_call(
        line_inputs_kernel,
        out_shape=[
            jax.ShapeDtypeStruct((STEPS, EQ, E), F32),
            jax.ShapeDtypeStruct((2, STEPS, SEL, E), F32),
            jax.ShapeDtypeStruct((2, STEPS, EQ, E), F32),
            jax.ShapeDtypeStruct((2, STEPS, EQ, E), F32),
            jax.ShapeDtypeStruct((STEPS, EQ, E), F32),
        ],
        in_specs=vmem(5),
        out_specs=vmem(5),
        scratch_shapes=[pltpu.VMEM((256, E), F32), pltpu.VMEM((256, E), F32), pltpu.VMEM((STEPS, EQ, E), F32)],
        compiler_params=PARAMS,
        name="z_inputs",
    )(values, table, lhsq, xp, gain2)


def z_lines(given, ready):
    table, _, _, wo, _ = ready
    return pl.pallas_call(
        line_scan_kernel,
        out_shape=jax.ShapeDtypeStruct((256, 2 * C), F32),
        in_specs=vmem(7),
        out_specs=vmem(1)[0],
        scratch_shapes=[pltpu.VMEM((STEPS, EQ, E), F32), pltpu.VMEM((STEPS, E, EQ), F32)],
        compiler_params=PARAMS,
        name="z_lines",
    )(table, wo, *given)


def local(voxels, norm_gain, in_weight, conv_weight, conv_bias, x_weight, dt_weight, dt_bias, a_rate, skip_gain, out_weight):
    pairs = voxels.reshape(2, 128, 2 * C)
    sent = pairs.transpose(1, 0, 2)
    arrived = lax.all_to_all(sent, ("row", "col"), split_axis=0, concat_axis=0, tiled=True)
    ready, z_ready = prepare(
        in_weight,
        conv_weight,
        conv_bias,
        x_weight.transpose(0, 2, 1),
        dt_weight,
        dt_bias,
        a_rate.transpose(0, 2, 1),
        skip_gain,
        out_weight.T,
        norm_gain.reshape(1, C),
    )
    given = z_inputs(pairs.reshape(256, 2 * C), z_ready)
    far = planes(arrived.reshape(256, 2 * C), ready)
    returned = lax.all_to_all(far.reshape(128, 2, 2 * C), ("row", "col"), split_axis=0, concat_axis=0, tiled=True)
    near = z_lines(given, z_ready)
    mixed = (near.reshape(128, 2, 2 * C) + returned.astype(F32)).astype(BF16)
    return mixed.transpose(1, 0, 2).reshape(1, 2, 128 * 2 * C)


def solution(mesh):
    in_specs = (P("row", "col", None),) + (P(),) * 10
    return jax.shard_map(local, mesh=mesh, in_specs=in_specs, out_specs=P("row", "col", None), check_vma=False)
```
